256 devices in a mesh: gz: 2 (over y_lo), gy: 8 (over x, core), gx: 16 (over z, y_hi).
Axes of the slice: x: 4, y: 4 (y_hi: 2, y_lo: 2; y = y_hi * 2 + y_lo), z: 8, core: 2. Of those that a mesh axis runs over, the one named last changes fastest.
Arguments:
- patches: bfloat16 [4, 32, 64, 128, 128], P('gz', 'gy', 'gx'), may hold values from -6 to 6
- prior_patches: bfloat16 [32, 64, 128, 128], P('gy', 'gx'), may hold values from -6 to 6
- node_patch: int32 [4, 128, 256], P(None, 'gy', 'gx'), may hold values from 0 to 35, as said below
- node_weight: float32 [4, 128, 256], P(None, 'gy', 'gx'), may hold values from 0.1 to 0.5
- edges: int32 [4, 128, 256], P(None, 'gy', 'gx'), may hold values from 0 to 1, as said below
- flow_weight: float32 [4, 128, 256], P('gz', 'gy', 'gx'), may hold values from 0.1 to 1
- start_offset: float32 [4, 2, 128, 256], P('gz', None, 'gy', 'gx'), may hold values from -6 to 6
Outputs:
- flow_field: float32 [4, 2, 32, 64], P('gz', None, 'gy', 'gx')
- displacement: float32 [4, 2, 128, 256], P('gz', None, 'gy', 'gx')
The draws below stay inside these ranges and needn't reach their ends.
Inputs may be any that keep to these rules, and one draw needn't show every extreme that they name: `node_patch`: for the node in row i and column j of its block of 16 x 16 nodes, every entry is (r + a) * 6 + c + b with r = 1 + i * 4 // 16, c = 1 + j * 4 // 16 and a, b each one of -1, 0, 1. `edges`: entry 1 of a node equals entry 0 of the node in the previous column, entry 3 equals entry 2 of the node in the previous row; springs that would leave the grid are 0.
All inputs are finite; a program needn't handle non-finite values.
Results may differ from the reference program's by a relative error of at most 0.0003.
Values may be sent and summed in bfloat16 or wider, within the bound.
No kernel may reach another device: no remote copies, remote signals or barrier semaphores. Data moves between devices by JAX's collectives and lax.ppermute only.
A program may use at most 64 MiB of HBM per device.

```python
import math
import jax
import jax.numpy as jnp
from jax import lax

P_SIZE = 128
PY = 4
PX = 4
STEPS = 3
MY = 16
MX = 16
SECTIONS = 4
NPYG = 32
NPXG = 64
NMY = 128
NMX = 256


def draw_node_patch(key, part):
    key = jax.random.fold_in(key, 11)
    first_key, second_key = jax.random.split(key)
    row_step = jax.random.randint(first_key, (4, NMY, NMX), -1, 2).astype(jnp.int32)
    col_step = jax.random.randint(second_key, (4, NMY, NMX), -1, 2).astype(jnp.int32)
    local_rows = jnp.arange(NMY, dtype=jnp.int32) % MY
    local_cols = jnp.arange(NMX, dtype=jnp.int32) % MX
    lowest = (local_rows == 0)[:, None] & (local_cols == 0)[None, :]
    highest = (local_rows == MY - 1)[:, None] & (local_cols == MX - 1)[None, :]
    row_first = jnp.where(highest, 1, jnp.where(lowest, -1, row_step[0]))
    col_first = jnp.where(highest, 1, jnp.where(lowest, -1, col_step[0]))
    row_step = row_step.at[0].set(row_first.astype(jnp.int32))
    col_step = col_step.at[0].set(col_first.astype(jnp.int32))
    base_row = (1 + local_rows * PY // MY)[None, :, None]
    base_col = (1 + local_cols * PX // MX)[None, None, :]
    return ((base_row + row_step) * (PX + 2) + base_col + col_step).astype(jnp.int32)


def draw_edges(key, part):
    key = jax.random.fold_in(key, 12)
    first_key, second_key = jax.random.split(key)
    right_links = (jax.random.randint(first_key, (NMY, NMX), 0, 8) > 0).astype(jnp.int32)
    right_links = right_links.at[:, NMX - 1].set(0)
    down_links = (jax.random.randint(second_key, (NMY, NMX), 0, 8) > 0).astype(jnp.int32)
    down_links = down_links.at[NMY - 1, :].set(0)
    left_links = jnp.concatenate([jnp.zeros((NMY, 1), jnp.int32), right_links[:, :-1]], axis=1)
    up_links = jnp.concatenate([jnp.zeros((1, NMX), jnp.int32), down_links[:-1, :]], axis=0)
    return jnp.stack([right_links, left_links, down_links, up_links]).astype(jnp.int32)


def block_scale(key, dims, cuts, smallest, high):
    level, own = 1.0, jax.random.fold_in(key, 6)
    for axis_at, shards_of in cuts:
        steps = jnp.exp(jax.random.uniform(jax.random.fold_in(own, axis_at), (shards_of,), jnp.float32, smallest / len(cuts), high / len(cuts)))
        level = level * jnp.repeat(steps, dims[axis_at] // shards_of).reshape([-1 if axis == axis_at else 1 for axis in range(len(dims))])
    return level


def normal_values(own_key, extent, spread, bound, cuts=(), kind=jnp.bfloat16):
    drawn = jax.random.normal(own_key, extent, jnp.float32) * spread
    if len(cuts) > 0:
        drawn = block_scale(own_key, extent, cuts, -0.22, 0.18) * drawn
    return jnp.clip(drawn, min=-bound, max=bound).astype(kind)


def setup_inputs(seed: int = 0) -> dict:
    seeds = jax.random.split(jax.random.key(seed), 8)
    return {
        "patches": normal_values(seeds[0], (SECTIONS, NPYG, NPXG, P_SIZE, P_SIZE), 1.0, 6.0, ((0, 2), (1, 8), (2, 16))),
        "prior_patches": normal_values(seeds[1], (NPYG, NPXG, P_SIZE, P_SIZE), 1.0, 6.0, ((0, 8), (1, 16))),
        "node_patch": draw_node_patch(jax.random.fold_in(seeds[7], 71), 0),
        "node_weight": jnp.clip(0.1 + 0.4 * jax.random.uniform(seeds[3], (4, NMY, NMX), jnp.float32) ** block_scale(seeds[3], (4, NMY, NMX), ((1, 8), (2, 16)), -0.2, 0.2), 0.1, 0.5),
        "edges": draw_edges(jax.random.fold_in(seeds[7], 71), 0),
        "flow_weight": jnp.clip(jnp.exp(math.log(1.0) - 2.3025851 * jax.random.uniform(seeds[5], (SECTIONS, NMY, NMX), jnp.float32) ** block_scale(seeds[5], (SECTIONS, NMY, NMX), ((0, 2), (1, 8), (2, 16)), -0.2, 0.2)), 0.1, 1.0),
        "start_offset": normal_values(seeds[6], (SECTIONS, 2, NMY, NMX), 1.0, 6.0, ((0, 2), (2, 8), (3, 16)), jnp.float32),
    }


def pair_flow(prev_row, cur_row):
    prev_spec = jnp.fft.fft2(prev_row.astype(jnp.float32))
    cur_spec = jnp.fft.fft2(cur_row.astype(jnp.float32))
    correlation = jnp.real(jnp.fft.ifft2(jnp.conj(prev_spec) * cur_spec))
    power_map = correlation * correlation
    offsets = ((jnp.arange(P_SIZE) + P_SIZE // 2) % P_SIZE - P_SIZE // 2).astype(jnp.float32)
    energy = jnp.mean(power_map, axis=(-2, -1)) + 1e-6
    along_y = jnp.mean(power_map * offsets[:, None], axis=(-2, -1)) / energy
    along_x = jnp.mean(power_map * offsets[None, :], axis=(-2, -1)) / energy
    return jnp.stack([along_y, along_x], axis=0)


def reference(patches, prior_patches, node_patch, node_weight, edges, flow_weight, start_offset):
    every_section = jnp.concatenate([prior_patches[None], patches], axis=0)

    def one_section(section):
        def one_row(row_index):
            return pair_flow(every_section[section, row_index], every_section[section + 1, row_index])
        return lax.map(one_row, jnp.arange(NPYG))

    flow_field = lax.map(one_section, jnp.arange(SECTIONS)).transpose(0, 2, 1, 3)
    padded_flow = jnp.pad(flow_field, ((0, 0), (0, 0), (1, 1), (1, 1)))
    grid_rows = ((jnp.arange(NMY) // MY) * PY).astype(jnp.int32)[None, :, None] + node_patch // (PX + 2)
    grid_cols = ((jnp.arange(NMX) // MX) * PX).astype(jnp.int32)[None, None, :] + node_patch % (PX + 2)
    gathered = padded_flow[:, :, grid_rows, grid_cols]
    target = jnp.sum(node_weight[None, None] * gathered, axis=2)
    links = edges.astype(jnp.float32)
    moved = start_offset
    for iteration in range(STEPS):
        padded = jnp.pad(moved, ((0, 0), (0, 0), (1, 1), (1, 1)))
        center = padded[..., 1:-1, 1:-1]
        springs = links[0] * (padded[..., 1:-1, 2:] - center) + links[1] * (padded[..., 1:-1, :-2] - center)
        springs = springs + links[2] * (padded[..., 2:, 1:-1] - center) + links[3] * (padded[..., :-2, 1:-1] - center)
        pulled = flow_weight[:, None] * (target - center)
        moved = center + 0.35 * (pulled + springs)
    return flow_field, moved
```

```python
import functools
import math

import jax
import jax.numpy as jnp
import ml_dtypes
import numpy as np
from jax import lax
from jax.experimental import pallas as pl
from jax.experimental.pallas import tpu as pltpu
from jax.sharding import PartitionSpec as P

STEPS = 3
STEP_SIZE = 0.35
N = 128
H = N // 2
F32 = jnp.float32
BF16 = jnp.bfloat16
GROUP = 32
EDGE = 3
VMEM_LIMIT = 40 * 1024 * 1024


def split_const(values):
    high = values.astype(ml_dtypes.bfloat16)
    low = (values - high.astype(np.float64)).astype(ml_dtypes.bfloat16)
    return high, low


@functools.lru_cache(maxsize=None)
def tables():
    pixel = np.arange(N)
    phase = 2.0 * np.pi / N * (np.outer(np.arange(H), pixel) % N)
    cosine, sine = np.cos(phase), np.sin(phase)
    sine[0] = np.cos(np.pi * pixel)
    norm = np.full(H, math.sqrt(2.0 / N))
    norm[0] = math.sqrt(1.0 / N)
    basis = np.concatenate([cosine * norm[:, None], sine * norm[:, None]])
    root = basis / np.sqrt(np.concatenate([norm, norm]))[:, None]
    wide = np.zeros((2 * N, 2 * N))
    wide[:N, 0:H], wide[:N, N : N + H] = root[:H].T, root[H:].T
    wide[N:, H:N], wide[N:, N + H :] = root[:H].T, root[H:].T
    back = np.zeros((2 * N, 2 * N))
    back[0:H, :N], back[N : N + H, :N] = basis[:H], basis[H:]
    back[H:N, N:], back[N + H :, N:] = basis[:H], basis[H:]
    offset = ((pixel + H) % N - H).astype(np.float64)
    moment = (basis * offset[None, :]) @ basis.T
    stacked = []
    for left in (root, moment):
        high, low = split_const(left)
        stacked.append(np.block([[high, high], [low, low]]))
    return (*split_const(wide), stacked[0], stacked[1], *split_const(back))


def dot(left, right):
    return jnp.dot(left, right, preferred_element_type=F32)


def halves(values):
    high = values.astype(BF16)
    return high, (values - high.astype(F32)).astype(BF16)


def left_product(stacked, values):
    high, low = halves(values)
    both = dot(stacked, jnp.concatenate([high, low], axis=0))
    return both[:N] + both[N:]


def spectrum(pixels, wide_high, wide_low, rows):
    return left_product(rows, dot(pixels, wide_high) + dot(pixels, wide_low))


def cross(prev, cur):
    lane = lax.broadcasted_iota(jnp.int32, (H, N), 1) % H == 0

    def part(start, stop, first_row):
        def quarter(whole, row, col):
            return whole[row + start : row + stop, col : col + N]

        pcc, pcs, psc, pss = (quarter(prev, r, c) for r in (0, H) for c in (0, N))
        qcc, qcs, qsc, qss = (quarter(cur, r, c) for r in (0, H) for c in (0, N))
        edge = lane[start:stop]
        u1, u2, u3, u4 = pcc * qcc, pss * qss, pcs * qcs, psc * qsc
        v1, v2, v3, v4 = pcc * qcs, pss * qsc, pcs * qcc, psc * qss
        w1, w2, w3, w4 = pcc * qsc, pss * qcs, pcs * qss, psc * qcc
        z = pcc * qss + pss * qcc - pcs * qsc - psc * qcs
        even, odd = u2 + u3, w3 - w2
        cc = u1 + u4 + jnp.where(edge, 0.0, even)
        cs = jnp.where(edge, even, (v1 - v3) + (v4 - v2))
        sc = (w1 - w4) + jnp.where(edge, 0.0, odd)
        ss = jnp.where(edge, odd, z)
        if first_row:
            top = lax.broadcasted_iota(jnp.int32, (stop - start, N), 0) == 0
            cc = jnp.where(top, u1 + jnp.where(edge, 0.0, u3), cc)
            cs = jnp.where(top, jnp.where(edge, u3, v1 - v3), cs)
            sc = jnp.where(top, u4 + jnp.where(edge, 0.0, u2), sc)
            ss = jnp.where(top, jnp.where(edge, u2, v4 - v2), ss)
        return jnp.concatenate([cc, cs], axis=1), jnp.concatenate([sc, ss], axis=1)

    first, rest = part(0, 8, True), part(8, H, False)
    return jnp.concatenate([first[0], rest[0], first[1], rest[1]], axis=0)


def moments(prev, cur, moment, back_high, back_low):
    values = cross(prev, cur)
    along_y = jnp.sum(values * left_product(moment, values), axis=0, keepdims=True)
    along_y = along_y[:, :N] + along_y[:, N:]
    high, low = halves(values)
    pixels = dot(high, back_high) + dot(low, back_high) + dot(high, back_low)
    return along_y, jnp.sum(pixels * pixels, axis=0, keepdims=True)


def placed_flows(along_y, power, section, first_col):
    lane = lax.broadcasted_iota(jnp.int32, (8, N), 1)
    offset = ((lane + H) % N - H).astype(F32)
    pad = jnp.zeros((2, N), F32)
    flows = jnp.zeros((8, N), F32)
    stacked_y = jnp.concatenate([pad, *along_y, pad], axis=0)
    for side in range(2):
        columns = jnp.concatenate([pad, *[p[:, side * N : (side + 1) * N] for p in power], pad], axis=0)
        energy = jnp.sum(columns, axis=1, keepdims=True) * (1.0 / (N * N)) + 1e-6
        mine = (lane < H) if side == 0 else (lane >= H)
        flow_y = jnp.sum(jnp.where(mine, stacked_y, 0.0), axis=1, keepdims=True) * (1.0 / (N * N)) / energy
        flow_x = jnp.sum(columns * offset, axis=1, keepdims=True) * (1.0 / (N * N)) / energy
        slot = section * 16 + 2 + first_col + side
        flows = jnp.where(lane == slot, flow_y, flows)
        flows = jnp.where(lane == slot + 8, flow_x, flows)
    return flows


def position(flags_ref):
    return [flags_ref[i] for i in range(7)]


def pair_of(ref, index):
    return jnp.concatenate([ref[(*index, 0)], ref[(*index, 1)]], axis=1)


def local_kernel(flags_ref, patches_ref, start_ref, weight_ref, edges_ref, nodes_ref, share_ref,
                 wide_high, wide_low, rows, moment, back_high, back_low, spec_ref, flows_ref, static_ref, sums_y, sums_x):
    odd = flags_ref[1]
    forward = (wide_high[...], wide_low[...], rows[...])
    inverse = (moment[...], back_high[...], back_low[...])
    static_ref[...] = jnp.zeros_like(static_ref)
    fields = [start_ref[s, c] for s in range(2) for c in range(2)]
    fields += [weight_ref[0], weight_ref[1], edges_ref[0].astype(F32), edges_ref[2].astype(F32)]
    fields += [nodes_ref[k].astype(F32) for k in range(4)] + [share_ref[k] for k in range(4)]
    for at, field in enumerate(fields):
        row, lane = at // 4 * 16, at % 4 * GROUP + EDGE
        static_ref[row : row + 16, lane : lane + 16] = field

    @pl.loop(0, 8)
    def _(unit):
        half, py = unit // 4, unit % 4
        first = 2 * (half ^ odd)
        pair = [jnp.concatenate([patches_ref[s, py, first], patches_ref[s, py, first + 1]], axis=1) for s in range(2)]
        prev, cur = (spectrum(p, *forward) for p in pair)
        spec_ref[half, py] = prev
        along_y, power = moments(prev, cur, *inverse)
        sums_y[unit] = along_y
        sums_x[unit] = power

    flows = jnp.zeros((8, N), F32)
    for half in range(2):
        flows += placed_flows([sums_y[half * 4 + i] for i in range(4)], [sums_x[half * 4 + i] for i in range(4)], 1, 2 * (half ^ odd))
    flows_ref[...] = flows


def chained_kernel(half, flags_ref, prior_ref, recv_ref, spec_ref, before_ref, static_ref,
                   wide_high, wide_low, rows, moment, back_high, back_low, out_ref, *field_ref):
    at_start, odd = flags_ref[0] == 0, flags_ref[1]
    forward = (wide_high[...], wide_low[...], rows[...])
    inverse = (moment[...], back_high[...], back_low[...])
    first = 2 * (half ^ odd)
    sums = []
    for py in range(4):
        own = jnp.concatenate([prior_ref[py, first], prior_ref[py, first + 1]], axis=1)
        other = jnp.concatenate([recv_ref[py, 0], recv_ref[py, 1]], axis=1)
        pixels = jnp.where(at_start, own, other)
        sums.append(moments(spectrum(pixels, *forward), spec_ref[py], *inverse))
    flows = before_ref[0:8, :] + placed_flows([s[0] for s in sums], [s[1] for s in sums], 0, first)
    out_ref[0:8, :] = flows
    out_ref[8:, :] = static_ref[...]
    if field_ref:
        for s in range(2):
            for c in range(2):
                lane = s * 16 + c * 8 + 2
                field_ref[0][s, c] = flows[2:6, lane : lane + 4]


def columns_kernel(flags_ref, own_ref, near_ref, far_ref, low_ref, high_ref):
    _, odd, has_left, has_right, odd_row, _, _ = position(flags_ref)
    own, near, far = own_ref[...], near_ref[...], far_ref[...]
    left = jnp.where(odd == 1, near, far) * has_left.astype(F32)
    right = jnp.where(odd == 1, far, near) * has_right.astype(F32)

    lane = lax.broadcasted_iota(jnp.int32, (8, N), 1) % 8
    flows = jnp.where(lane < 2, pltpu.roll(left[:8], N - 4, 1), jnp.where(lane < 6, own[:8], pltpu.roll(right[:8], 4, 1)))
    lane = lax.broadcasted_iota(jnp.int32, (64, N), 1) % GROUP
    nodes = jnp.where(lane < EDGE, pltpu.roll(left[8:], N - 16, 1),
                      jnp.where(lane < EDGE + 16, own[8:], jnp.where(lane < 2 * EDGE + 16, pltpu.roll(right[8:], 16, 1), 0.0)))
    top = jnp.concatenate([flows] + [nodes[16 * f : 16 * f + 8] for f in range(4)], axis=0)
    bottom = jnp.concatenate([flows] + [nodes[16 * f + 8 : 16 * f + 16] for f in range(4)], axis=0)
    low_ref[...] = top
    high_ref[...] = bottom


def shifted_rows(values, by):
    return pltpu.roll(values, by % values.shape[0], 0)


def nodes_kernel(flags_ref, top_ref, bottom_ref, near_ref, far_ref, spread_ref, out_ref):
    _, _, _, _, odd_row, has_up, has_down = position(flags_ref)
    top, bottom, near, far = top_ref[...], bottom_ref[...], near_ref[...], far_ref[...]
    above = jnp.where(odd_row == 1, near, far) * has_up.astype(F32)
    below = jnp.where(odd_row == 1, far, near) * has_down.astype(F32)

    row = lax.broadcasted_iota(jnp.int32, (8, N), 0)
    window = jnp.where(row < 2, pltpu.roll(above[:8], 4, 0), jnp.where(row < 6, top[:8], pltpu.roll(below[:8], 4, 0)))

    def field(at):
        part = slice(8 + 8 * at, 16 + 8 * at)
        return jnp.concatenate([above[part], top[part], bottom[part], below[part]], axis=0)

    moved, mixed, patch, share = (field(at) for at in range(4))

    narrow = window[:, : 4 * 8]
    part1 = narrow.astype(BF16)
    rest = narrow - part1.astype(F32)
    part2 = rest.astype(BF16)
    part3 = (rest - part2.astype(F32)).astype(BF16)
    spread = dot(jnp.concatenate([part1, part2, part3], axis=1), spread_ref[...])
    upper = row < 4
    lines = [[jnp.broadcast_to(spread[r : r + 1, b * N : (b + 1) * N], (8, N)) for b in range(3)] for r in range(8)]

    def patch_row(r):
        return lines[min(max(r, 0), 7)]

    rows4 = lax.broadcasted_iota(jnp.int32, (32, N), 0)
    lanes4 = lax.broadcasted_iota(jnp.int32, (32, N), 1)
    base = (1 + (rows4 + 8) % 16 // 4) * 6 + 1 + (lanes4 % GROUP + 16 - EDGE) % 16 // 4
    step = patch - base.astype(F32)

    def over_groups(values):
        values = values + pltpu.roll(values, GROUP, 1)
        return values + pltpu.roll(values, 2 * GROUP, 1)

    target = jnp.zeros((32, N), F32)
    for a in range(-1, 2):
        for b in range(-1, 2):
            weight = over_groups(jnp.where(step == float(6 * a + b), share, 0.0))
            moving = jnp.concatenate([jnp.where(upper, patch_row(2 * t + a)[b + 1], patch_row(2 * t + 1 + a)[b + 1]) for t in range(4)], axis=0)
            target = target + weight * moving

    group = lanes4 // GROUP
    stiff_pair = jnp.where(group < 2, mixed, 0.0)
    only0 = jnp.where(group == 0, mixed, 0.0)
    only1 = jnp.where(group == 1, mixed, 0.0)
    stiffness = only0 + pltpu.roll(only0, GROUP, 1) + pltpu.roll(only1, GROUP, 1) + pltpu.roll(only1, 2 * GROUP, 1)
    right = over_groups(jnp.where(group == 2, mixed, 0.0))
    down = over_groups(jnp.where(group == 3, mixed, 0.0))
    left = pltpu.roll(right, 1, 1)
    up = shifted_rows(down, 1)
    for _ in range(STEPS):
        springs = right * (pltpu.roll(moved, N - 1, 1) - moved) + left * (pltpu.roll(moved, 1, 1) - moved)
        springs = springs + down * (shifted_rows(moved, -1) - moved) + up * (shifted_rows(moved, 1) - moved)
        moved = moved + STEP_SIZE * (stiffness * (target - moved) + springs)
    for s in range(2):
        for c in range(2):
            lane = (2 * s + c) * GROUP + EDGE
            out_ref[s, c] = moved[8:24, lane : lane + 16]


@functools.lru_cache(maxsize=None)
def spread_table():
    table = np.zeros((3, 32, 3 * N))
    for b in range(3):
        for lane in range(N):
            group, node = lane // GROUP, lane % GROUP - EDGE
            col = node // 4 + 2 + b - 1
            if 0 <= col < 8 and node < 19:
                table[:, group * 8 + col, b * N + lane] = 1.0
    return table.reshape(96, 3 * N).astype(ml_dtypes.bfloat16)


def call(kernel, inputs, out_shapes, scratch=(), flops=0, moved=0):
    return pl.pallas_call(
        kernel,
        out_shape=out_shapes,
        in_specs=[pl.BlockSpec(memory_space=pltpu.SMEM)] + [pl.BlockSpec(memory_space=pltpu.VMEM)] * (len(inputs) - 1),
        out_specs=jax.tree.map(lambda _: pl.BlockSpec(memory_space=pltpu.VMEM), out_shapes),
        scratch_shapes=scratch,
        compiler_params=pltpu.CompilerParams(vmem_limit_bytes=VMEM_LIMIT),
        cost_estimate=pl.CostEstimate(flops=flops, bytes_accessed=moved, transcendentals=0),
    )(*inputs)


def f32(*shape):
    return jax.ShapeDtypeStruct(shape, F32)


def near_partner(count):
    return [(i, i ^ 1) for i in range(count)]


def far_partner(count):
    pairs = []
    for i in range(count):
        other = i + 1 if i % 2 else i - 1
        pairs.append((i, other if 0 <= other < count else i))
    return pairs


def body(patches, prior_patches, node_patch, node_weight, edges, flow_weight, start_offset):
    gz, gy, gx = (lax.axis_index(a) for a in ("gz", "gy", "gx"))
    rows, cols = lax.axis_size("gy"), lax.axis_size("gx")
    odd = gx % 2
    flags = jnp.stack([gz, odd, gx > 0, gx < cols - 1, gy % 2, gy > 0, gy < rows - 1]).astype(jnp.int32)
    consts = [jnp.asarray(t) for t in tables()]
    along_z = [(0, 1)]

    last = patches[1]
    arriving = []
    for half in range(2):
        chunk = lax.dynamic_slice_in_dim(last, 2 * (half ^ odd), 2, axis=1)
        arriving.append(lax.ppermute(chunk, "gz", along_z))

    spec, flows, static = call(
        local_kernel,
        [flags, patches, start_offset, flow_weight, edges, node_patch, node_weight, *consts],
        [f32(2, 4, N, 2 * N), f32(8, N), f32(64, N)],
        scratch=[pltpu.VMEM((8, 1, N), F32), pltpu.VMEM((8, 1, 2 * N), F32)],
        flops=5_000_000_000, moved=4_000_000,
    )
    (first,) = call(
        functools.partial(chained_kernel, 0),
        [flags, prior_patches, arriving[0], spec[0], flows, static, *consts],
        [f32(72, N)], flops=1_000_000_000, moved=2_000_000,
    )
    from_far = lax.ppermute(first, "gx", far_partner(cols))
    own, flow_field = call(
        functools.partial(chained_kernel, 1),
        [flags, prior_patches, arriving[1], spec[1], first, static, *consts],
        [f32(72, N), f32(2, 2, 4, 4)], flops=1_000_000_000, moved=2_000_000,
    )
    from_near = lax.ppermute(own, "gx", near_partner(cols))
    top, bottom = call(columns_kernel, [flags, own, from_near, from_far], [f32(40, N), f32(40, N)])
    odd_row = flags[4] == 1
    to_near = jnp.where(odd_row, top, bottom)
    to_far = jnp.where(odd_row, bottom, top)
    row_near = lax.ppermute(to_near, "gy", near_partner(rows))
    row_far = lax.ppermute(to_far, "gy", far_partner(rows))
    displacement = call(
        nodes_kernel, [flags, top, bottom, row_near, row_far, jnp.asarray(spread_table())], f32(2, 2, 16, 16))
    return flow_field, displacement


def solution(mesh):
    return jax.shard_map(
        body,
        mesh=mesh,
        in_specs=(
            P("gz", "gy", "gx", None, None),
            P("gy", "gx", None, None),
            P(None, "gy", "gx"),
            P(None, "gy", "gx"),
            P(None, "gy", "gx"),
            P("gz", "gy", "gx"),
            P("gz", None, "gy", "gx"),
        ),
        out_specs=(P("gz", None, "gy", "gx"), P("gz", None, "gy", "gx")),
        check_vma=False,
    )
```

```python
import functools
import math

import jax
import jax.numpy as jnp
import ml_dtypes
import numpy as np
from jax import lax
from jax.experimental import pallas as pl
from jax.experimental.pallas import tpu as pltpu
from jax.sharding import PartitionSpec as P

STEPS = 3
STEP_SIZE = 0.35
N = 128
H = N // 2
F32 = jnp.float32
BF16 = jnp.bfloat16
GROUP = 32
EDGE = 3
VMEM_LIMIT = 24 * 1024 * 1024


def split_const(values):
    high = values.astype(ml_dtypes.bfloat16)
    low = (values - high.astype(np.float64)).astype(ml_dtypes.bfloat16)
    return high, low


@functools.lru_cache(maxsize=None)
def tables():
    pixel = np.arange(N)
    phase = 2.0 * np.pi / N * (np.outer(np.arange(H), pixel) % N)
    cosine, sine = np.cos(phase), np.sin(phase)
    sine[0] = np.cos(np.pi * pixel)
    norm = np.full(H, math.sqrt(2.0 / N))
    norm[0] = math.sqrt(1.0 / N)
    basis = np.concatenate([cosine * norm[:, None], sine * norm[:, None]])
    root = basis / np.sqrt(np.concatenate([norm, norm]))[:, None]
    wide = np.zeros((2 * N, 2 * N))
    wide[:N, 0:H], wide[:N, N : N + H] = root[:H].T, root[H:].T
    wide[N:, H:N], wide[N:, N + H :] = root[:H].T, root[H:].T
    back = np.zeros((2 * N, 2 * N))
    back[0:H, :N], back[N : N + H, :N] = basis[:H], basis[H:]
    back[H:N, N:], back[N + H :, N:] = basis[:H], basis[H:]
    offset = ((pixel + H) % N - H).astype(np.float64)
    moment = (basis * offset[None, :]) @ basis.T
    stacked = []
    for left in (root, moment):
        high, low = split_const(left)
        stacked.append(np.block([[high, high], [low, low]]))
    return np.stack([*split_const(wide), stacked[0], stacked[1], *split_const(back)])


def dot(left, right):
    return jnp.dot(left, right, preferred_element_type=F32)


def halves(values):
    high = values.astype(BF16)
    return high, (values - high.astype(F32)).astype(BF16)


def left_product(stacked, values):
    high, low = halves(values)
    both = dot(stacked, jnp.concatenate([high, low], axis=0))
    return both[:N] + both[N:]


def spectrum(pixels, wide_high, wide_low, rows):
    return left_product(rows, dot(pixels, wide_high) + dot(pixels, wide_low))


def cross(prev, cur):
    lane = lax.broadcasted_iota(jnp.int32, (H, N), 1) % H == 0

    def part(start, stop, first_row):
        def quarter(whole, row, col):
            return whole[row + start : row + stop, col : col + N]

        pcc, pcs, psc, pss = (quarter(prev, r, c) for r in (0, H) for c in (0, N))
        qcc, qcs, qsc, qss = (quarter(cur, r, c) for r in (0, H) for c in (0, N))
        edge = lane[start:stop]
        u1, u2, u3, u4 = pcc * qcc, pss * qss, pcs * qcs, psc * qsc
        v1, v2, v3, v4 = pcc * qcs, pss * qsc, pcs * qcc, psc * qss
        w1, w2, w3, w4 = pcc * qsc, pss * qcs, pcs * qss, psc * qcc
        z = pcc * qss + pss * qcc - pcs * qsc - psc * qcs
        even, odd = u2 + u3, w3 - w2
        cc = u1 + u4 + jnp.where(edge, 0.0, even)
        cs = jnp.where(edge, even, (v1 - v3) + (v4 - v2))
        sc = (w1 - w4) + jnp.where(edge, 0.0, odd)
        ss = jnp.where(edge, odd, z)
        if first_row:
            top = lax.broadcasted_iota(jnp.int32, (stop - start, N), 0) == 0
            cc = jnp.where(top, u1 + jnp.where(edge, 0.0, u3), cc)
            cs = jnp.where(top, jnp.where(edge, u3, v1 - v3), cs)
            sc = jnp.where(top, u4 + jnp.where(edge, 0.0, u2), sc)
            ss = jnp.where(top, jnp.where(edge, u2, v4 - v2), ss)
        return jnp.concatenate([cc, cs], axis=1), jnp.concatenate([sc, ss], axis=1)

    first, rest = part(0, 8, True), part(8, H, False)
    return jnp.concatenate([first[0], rest[0], first[1], rest[1]], axis=0)


def moments(prev, cur, moment, back_high, back_low):
    values = cross(prev, cur)
    along_y = jnp.sum(values * left_product(moment, values), axis=0, keepdims=True)
    along_y = along_y[:, :N] + along_y[:, N:]
    high, low = halves(values)
    pixels = dot(high, back_high) + dot(low, back_high) + dot(high, back_low)
    return along_y, jnp.sum(pixels * pixels, axis=0, keepdims=True)


def placed_flows(along_y, power, section, first_col):
    lane = lax.broadcasted_iota(jnp.int32, (8, N), 1)
    offset = ((lane + H) % N - H).astype(F32)
    pad = jnp.zeros((2, N), F32)
    flows = jnp.zeros((8, N), F32)
    stacked_y = jnp.concatenate([pad, *along_y, pad], axis=0)
    for side in range(2):
        columns = jnp.concatenate([pad, *[p[:, side * N : (side + 1) * N] for p in power], pad], axis=0)
        energy = jnp.sum(columns, axis=1, keepdims=True) * (1.0 / (N * N)) + 1e-6
        mine = (lane < H) if side == 0 else (lane >= H)
        flow_y = jnp.sum(jnp.where(mine, stacked_y, 0.0), axis=1, keepdims=True) * (1.0 / (N * N)) / energy
        flow_x = jnp.sum(columns * offset, axis=1, keepdims=True) * (1.0 / (N * N)) / energy
        slot = section * 16 + 2 + first_col + side
        flows = jnp.where(lane == slot, flow_y, flows)
        flows = jnp.where(lane == slot + 8, flow_x, flows)
    return flows


def local_kernel(flags_ref, patches_ref, start_ref, weight_ref, edges_ref, nodes_ref, share_ref,
                 table_ref, spec_ref, flows_ref, static_ref, current, sums_y, sums_x):
    odd = flags_ref[1]
    forward = [table_ref[i] for i in range(3)]
    inverse = [table_ref[i] for i in range(3, 6)]
    static_ref[...] = jnp.zeros_like(static_ref)
    fields = [start_ref[s, c] for s in range(2) for c in range(2)]
    fields += [weight_ref[0], weight_ref[1], edges_ref[0].astype(F32), edges_ref[2].astype(F32)]
    fields += [nodes_ref[k].astype(F32) for k in range(4)] + [share_ref[k] for k in range(4)]
    for at, field in enumerate(fields):
        row, lane = at // 4 * 16, at % 4 * GROUP + EDGE
        static_ref[row : row + 16, lane : lane + 16] = field

    for unit in range(8):
        half, py = unit // 4, unit % 4
        first = 2 * (half ^ odd)
        for section, result in ((0, spec_ref.at[half, py]), (1, current.at[unit])):
            pixels = jnp.concatenate([patches_ref[section, py, first], patches_ref[section, py, first + 1]], axis=1)
            result[...] = spectrum(pixels, *forward)
    for unit in range(8):
        along_y, power = moments(spec_ref[unit // 4, unit % 4], current[unit], *inverse)
        sums_y[unit] = along_y
        sums_x[unit] = power

    flows = jnp.zeros((8, N), F32)
    for half in range(2):
        flows += placed_flows([sums_y[half * 4 + i] for i in range(4)], [sums_x[half * 4 + i] for i in range(4)], 1, 2 * (half ^ odd))
    flows_ref[...] = flows


def chained_kernel(half, flags_ref, prior_ref, recv_ref, spec_ref, before_ref, static_ref, table_ref, out_ref, *rest):
    *field_ref, previous = rest
    at_start, odd = flags_ref[0] == 0, flags_ref[1]
    forward = [table_ref[i] for i in range(3)]
    inverse = [table_ref[i] for i in range(3, 6)]
    first = 2 * (half ^ odd)
    for py in range(4):
        own = jnp.concatenate([prior_ref[py, first], prior_ref[py, first + 1]], axis=1)
        other = jnp.concatenate([recv_ref[py, 0], recv_ref[py, 1]], axis=1)
        previous[py] = spectrum(jnp.where(at_start, own, other), *forward)
    sums = [moments(previous[py], spec_ref[py], *inverse) for py in range(4)]
    flows = before_ref[0:8, :] + placed_flows([s[0] for s in sums], [s[1] for s in sums], 0, first)
    out_ref[0:8, :] = flows
    out_ref[8:, :] = static_ref[...]
    if field_ref:
        for s in range(2):
            for c in range(2):
                lane = s * 16 + c * 8 + 2
                field_ref[0][s, c] = flows[2:6, lane : lane + 4]


def beside(base, values, on_right):
    lane = lax.broadcasted_iota(jnp.int32, (8, N), 1) % 8
    left = jnp.where(lane < 2, pltpu.roll(values[:8], N - 4, 1), base[:8])
    right = jnp.where(lane >= 6, pltpu.roll(values[:8], 4, 1), base[:8])
    flows = jnp.where(on_right, right, left)
    lane = lax.broadcasted_iota(jnp.int32, (64, N), 1) % GROUP
    left = jnp.where(lane < EDGE, pltpu.roll(values[8:], N - 16, 1), base[8:])
    right = jnp.where((lane >= EDGE + 16) & (lane < 2 * EDGE + 16), pltpu.roll(values[8:], 16, 1), base[8:])
    return flows, jnp.where(on_right, right, left)


def far_columns_kernel(flags_ref, static_ref, far_ref, out_ref):
    base = jnp.concatenate([jnp.zeros((8, N), F32), static_ref[...]], axis=0)
    flows, nodes = beside(base, far_ref[...] * flags_ref[2].astype(F32), flags_ref[1] == 1)
    out_ref[0:8, :] = flows
    out_ref[8:, :] = nodes


def near_columns_kernel(flags_ref, own_ref, partial_ref, near_ref, to_near_ref, to_far_ref):
    base = jnp.concatenate([partial_ref[0:8, :] + own_ref[0:8, :], partial_ref[8:, :]], axis=0)
    flows, nodes = beside(base, near_ref[...], flags_ref[1] == 0)
    top = jnp.concatenate([flows] + [nodes[16 * f : 16 * f + 8] for f in range(4)], axis=0)
    bottom = jnp.concatenate([flows] + [nodes[16 * f + 8 : 16 * f + 16] for f in range(4)], axis=0)
    odd = flags_ref[3] == 1
    to_near_ref[...] = jnp.where(odd, top, bottom)
    to_far_ref[...] = jnp.where(odd, bottom, top)


def shifted_rows(values, by):
    return pltpu.roll(values, by % values.shape[0], 0)


def nodes_kernel(flags_ref, to_near_ref, to_far_ref, near_ref, far_ref, spread_ref, out_ref):
    odd = flags_ref[3] == 1
    near, far = near_ref[...], far_ref[...] * flags_ref[4].astype(F32)
    above, below = jnp.where(odd, near, far), jnp.where(odd, far, near)
    top = jnp.where(odd, to_near_ref[...], to_far_ref[...])
    bottom = jnp.where(odd, to_far_ref[...], to_near_ref[...])

    row = lax.broadcasted_iota(jnp.int32, (8, N), 0)
    window = jnp.where(row < 2, pltpu.roll(above[:8], 4, 0), jnp.where(row < 6, top[:8], pltpu.roll(below[:8], 4, 0)))

    def field(at):
        part = slice(8 + 8 * at, 16 + 8 * at)
        return jnp.concatenate([above[part], top[part], bottom[part], below[part]], axis=0)

    moved, mixed, patch, share = (field(at) for at in range(4))

    narrow = window[:, : 4 * 8]
    part1 = narrow.astype(BF16)
    rest = narrow - part1.astype(F32)
    part2 = rest.astype(BF16)
    part3 = (rest - part2.astype(F32)).astype(BF16)
    spread = dot(jnp.concatenate([part1, part2, part3], axis=1), spread_ref[...])
    upper = row < 4
    lines = [[jnp.broadcast_to(spread[r : r + 1, b * N : (b + 1) * N], (8, N)) for b in range(3)] for r in range(8)]

    def patch_row(r):
        return lines[min(max(r, 0), 7)]

    rows4 = lax.broadcasted_iota(jnp.int32, (32, N), 0)
    lanes4 = lax.broadcasted_iota(jnp.int32, (32, N), 1)
    base = (1 + (rows4 + 8) % 16 // 4) * 6 + 1 + (lanes4 % GROUP + 16 - EDGE) % 16 // 4
    step = patch - base.astype(F32)

    def over_groups(values):
        values = values + pltpu.roll(values, GROUP, 1)
        return values + pltpu.roll(values, 2 * GROUP, 1)

    target = jnp.zeros((32, N), F32)
    for a in range(-1, 2):
        for b in range(-1, 2):
            weight = over_groups(jnp.where(step == float(6 * a + b), share, 0.0))
            moving = jnp.concatenate([jnp.where(upper, patch_row(2 * t + a)[b + 1], patch_row(2 * t + 1 + a)[b + 1]) for t in range(4)], axis=0)
            target = target + weight * moving

    group = lanes4 // GROUP
    stiff_pair = jnp.where(group < 2, mixed, 0.0)
    only0 = jnp.where(group == 0, mixed, 0.0)
    only1 = jnp.where(group == 1, mixed, 0.0)
    stiffness = only0 + pltpu.roll(only0, GROUP, 1) + pltpu.roll(only1, GROUP, 1) + pltpu.roll(only1, 2 * GROUP, 1)
    right = over_groups(jnp.where(group == 2, mixed, 0.0))
    down = over_groups(jnp.where(group == 3, mixed, 0.0))
    left = pltpu.roll(right, 1, 1)
    up = shifted_rows(down, 1)
    for _ in range(STEPS):
        springs = right * (pltpu.roll(moved, N - 1, 1) - moved) + left * (pltpu.roll(moved, 1, 1) - moved)
        springs = springs + down * (shifted_rows(moved, -1) - moved) + up * (shifted_rows(moved, 1) - moved)
        moved = moved + STEP_SIZE * (stiffness * (target - moved) + springs)
    for s in range(2):
        for c in range(2):
            lane = (2 * s + c) * GROUP + EDGE
            out_ref[s, c] = moved[8:24, lane : lane + 16]


@functools.lru_cache(maxsize=None)
def spread_table():
    table = np.zeros((3, 32, 3 * N))
    for b in range(3):
        for lane in range(N):
            group, node = lane // GROUP, lane % GROUP - EDGE
            col = node // 4 + 2 + b - 1
            if 0 <= col < 8 and node < 19:
                table[:, group * 8 + col, b * N + lane] = 1.0
    return table.reshape(96, 3 * N).astype(ml_dtypes.bfloat16)


def call(kernel, inputs, out_shapes, scratch=(), flops=0, moved=0):
    return pl.pallas_call(
        kernel,
        out_shape=out_shapes,
        in_specs=[pl.BlockSpec(memory_space=pltpu.SMEM)] + [pl.BlockSpec(memory_space=pltpu.VMEM)] * (len(inputs) - 1),
        out_specs=jax.tree.map(lambda _: pl.BlockSpec(memory_space=pltpu.VMEM), out_shapes),
        scratch_shapes=scratch,
        compiler_params=pltpu.CompilerParams(vmem_limit_bytes=VMEM_LIMIT),
        cost_estimate=pl.CostEstimate(flops=flops, bytes_accessed=moved, transcendentals=0),
    )(*inputs)


def f32(*shape):
    return jax.ShapeDtypeStruct(shape, F32)


def near_partner(count):
    return [(i, i ^ 1) for i in range(count)]


def far_partner(count):
    pairs = []
    for i in range(count):
        other = i + 1 if i % 2 else i - 1
        pairs.append((i, other if 0 <= other < count else i))
    return pairs


def body(patches, prior_patches, node_patch, node_weight, edges, flow_weight, start_offset):
    gz, gy, gx = (lax.axis_index(a) for a in ("gz", "gy", "gx"))
    rows, cols = lax.axis_size("gy"), lax.axis_size("gx")
    odd, odd_row = gx % 2, gy % 2
    has_far = (gx > 0) & (gx < cols - 1)
    has_far_row = (gy > 0) & (gy < rows - 1)
    flags = jnp.stack([gz, odd, has_far, odd_row, has_far_row]).astype(jnp.int32)
    table = jnp.asarray(tables())

    arriving = []
    for half in range(2):
        chunk = lax.dynamic_slice_in_dim(patches[1], 2 * (half ^ odd), 2, axis=1)
        arriving.append(lax.ppermute(chunk, "gz", [(0, 1)]))

    spec, flows, static = call(
        local_kernel,
        [flags, patches, start_offset, flow_weight, edges, node_patch, node_weight, table],
        [f32(2, 4, N, 2 * N), f32(8, N), f32(64, N)],
        scratch=[pltpu.VMEM((8, N, 2 * N), F32), pltpu.VMEM((8, 1, N), F32), pltpu.VMEM((8, 1, 2 * N), F32)],
        flops=5_000_000_000, moved=4_000_000,
    )
    scratch = [pltpu.VMEM((4, N, 2 * N), F32)]
    (first,) = call(
        functools.partial(chained_kernel, 0),
        [flags, prior_patches, arriving[0], spec[0], flows, static, table],
        [f32(72, N)], scratch, flops=2_000_000_000, moved=2_000_000,
    )
    from_far = lax.ppermute(first, "gx", far_partner(cols))
    partial = call(far_columns_kernel, [flags, static, from_far], f32(72, N), flops=5_000_000_000, moved=2_000_000)
    own, flow_field = call(
        functools.partial(chained_kernel, 1),
        [flags, prior_patches, arriving[1], spec[1], first, static, table],
        [f32(72, N), f32(2, 2, 4, 4)], scratch, flops=2_000_000_000, moved=2_000_000,
    )
    from_near = lax.ppermute(own, "gx", near_partner(cols))
    to_near, to_far = call(near_columns_kernel, [flags, own, partial, from_near], [f32(40, N), f32(40, N)])
    row_near = lax.ppermute(to_near, "gy", near_partner(rows))
    row_far = lax.ppermute(to_far, "gy", far_partner(rows))
    displacement = call(
        nodes_kernel, [flags, to_near, to_far, row_near, row_far, jnp.asarray(spread_table())], f32(2, 2, 16, 16))
    return flow_field, displacement


def solution(mesh):
    return jax.shard_map(
        body,
        mesh=mesh,
        in_specs=(
            P("gz", "gy", "gx", None, None),
            P("gy", "gx", None, None),
            P(None, "gy", "gx"),
            P(None, "gy", "gx"),
            P(None, "gy", "gx"),
            P("gz", "gy", "gx"),
            P("gz", None, "gy", "gx"),
        ),
        out_specs=(P("gz", None, "gy", "gx"), P("gz", None, "gy", "gx")),
        check_vma=False,
    )
```

```python
import functools
import math

import jax
import jax.numpy as jnp
import ml_dtypes
import numpy as np
from jax import lax
from jax.experimental import pallas as pl
from jax.experimental.pallas import tpu as pltpu
from jax.sharding import PartitionSpec as P

STEPS = 3
STEP_SIZE = 0.35
N = 128
H = N // 2
F32 = jnp.float32
BF16 = jnp.bfloat16
GROUP = 32
EDGE = 3
VMEM_LIMIT = 24 * 1024 * 1024


def split_const(values):
    high = values.astype(ml_dtypes.bfloat16)
    low = (values - high.astype(np.float64)).astype(ml_dtypes.bfloat16)
    return high, low


@functools.lru_cache(maxsize=None)
def tables():
    pixel = np.arange(N)
    phase = 2.0 * np.pi / N * (np.outer(np.arange(H), pixel) % N)
    cosine, sine = np.cos(phase), np.sin(phase)
    sine[0] = np.cos(np.pi * pixel)
    norm = np.full(H, math.sqrt(2.0 / N))
    norm[0] = math.sqrt(1.0 / N)
    basis = np.concatenate([cosine * norm[:, None], sine * norm[:, None]])
    root = basis / np.sqrt(np.concatenate([norm, norm]))[:, None]
    wide = np.zeros((2 * N, 2 * N))
    wide[:N, 0:H], wide[:N, N : N + H] = root[:H].T, root[H:].T
    wide[N:, H:N], wide[N:, N + H :] = root[:H].T, root[H:].T
    back = np.zeros((2 * N, 2 * N))
    back[0:H, :N], back[N : N + H, :N] = basis[:H], basis[H:]
    back[H:N, N:], back[N + H :, N:] = basis[:H], basis[H:]
    offset = ((pixel + H) % N - H).astype(np.float64)
    moment = (basis * offset[None, :]) @ basis.T
    stacked = []
    for left in (root, moment):
        high, low = split_const(left)
        stacked.append(np.block([[high, high], [low, low]]))
    return np.stack([*split_const(wide), stacked[0], stacked[1], *split_const(back)])


def dot(left, right):
    return jnp.dot(left, right, preferred_element_type=F32)


def halves(values):
    high = values.astype(BF16)
    return high, (values - high.astype(F32)).astype(BF16)


def left_product(stacked, values):
    high, low = halves(values)
    both = dot(stacked, jnp.concatenate([high, low], axis=0))
    return both[:N] + both[N:]


def spectrum(pixels, wide_high, wide_low, rows):
    return left_product(rows, dot(pixels, wide_high) + dot(pixels, wide_low))


def cross(prev, cur):
    lane = lax.broadcasted_iota(jnp.int32, (H, N), 1) % H == 0

    def part(start, stop, first_row):
        def quarter(whole, row, col):
            return whole[row + start : row + stop, col : col + N]

        pcc, pcs, psc, pss = (quarter(prev, r, c) for r in (0, H) for c in (0, N))
        qcc, qcs, qsc, qss = (quarter(cur, r, c) for r in (0, H) for c in (0, N))
        edge = lane[start:stop]
        u1, u2, u3, u4 = pcc * qcc, pss * qss, pcs * qcs, psc * qsc
        v1, v2, v3, v4 = pcc * qcs, pss * qsc, pcs * qcc, psc * qss
        w1, w2, w3, w4 = pcc * qsc, pss * qcs, pcs * qss, psc * qcc
        z = pcc * qss + pss * qcc - pcs * qsc - psc * qcs
        even, odd = u2 + u3, w3 - w2
        cc = u1 + u4 + jnp.where(edge, 0.0, even)
        cs = jnp.where(edge, even, (v1 - v3) + (v4 - v2))
        sc = (w1 - w4) + jnp.where(edge, 0.0, odd)
        ss = jnp.where(edge, odd, z)
        if first_row:
            top = lax.broadcasted_iota(jnp.int32, (stop - start, N), 0) == 0
            cc = jnp.where(top, u1 + jnp.where(edge, 0.0, u3), cc)
            cs = jnp.where(top, jnp.where(edge, u3, v1 - v3), cs)
            sc = jnp.where(top, u4 + jnp.where(edge, 0.0, u2), sc)
            ss = jnp.where(top, jnp.where(edge, u2, v4 - v2), ss)
        return jnp.concatenate([cc, cs], axis=1), jnp.concatenate([sc, ss], axis=1)

    first, rest = part(0, 8, True), part(8, H, False)
    return jnp.concatenate([first[0], rest[0], first[1], rest[1]], axis=0)


def moments(prev, cur, moment, back_high, back_low):
    values = cross(prev, cur)
    along_y = jnp.sum(values * left_product(moment, values), axis=0, keepdims=True)
    along_y = along_y[:, :N] + along_y[:, N:]
    high, low = halves(values)
    pixels = dot(high, back_high) + dot(low, back_high) + dot(high, back_low)
    return along_y, jnp.sum(pixels * pixels, axis=0, keepdims=True)


def placed_flows(along_y, power, section, first_col):
    lane = lax.broadcasted_iota(jnp.int32, (8, N), 1)
    offset = ((lane + H) % N - H).astype(F32)
    pad = jnp.zeros((2, N), F32)
    flows = jnp.zeros((8, N), F32)
    stacked_y = jnp.concatenate([pad, *along_y, pad], axis=0)
    for side in range(2):
        columns = jnp.concatenate([pad, *[p[:, side * N : (side + 1) * N] for p in power], pad], axis=0)
        energy = jnp.sum(columns, axis=1, keepdims=True) * (1.0 / (N * N)) + 1e-6
        mine = (lane < H) if side == 0 else (lane >= H)
        flow_y = jnp.sum(jnp.where(mine, stacked_y, 0.0), axis=1, keepdims=True) * (1.0 / (N * N)) / energy
        flow_x = jnp.sum(columns * offset, axis=1, keepdims=True) * (1.0 / (N * N)) / energy
        slot = section * 16 + 2 + first_col + side
        flows = jnp.where(lane == slot, flow_y, flows)
        flows = jnp.where(lane == slot + 8, flow_x, flows)
    return flows


def local_kernel(flags_ref, patches_ref, table_ref, spec0_ref, spec1_ref, flows_ref, later_ref, current, sums_y, sums_x):
    odd = flags_ref[1]
    forward = [table_ref[i] for i in range(3)]
    inverse = [table_ref[i] for i in range(3, 6)]
    for py in range(4):
        for j in range(2):
            later_ref[py, j] = patches_ref[1, py, 2 * (1 ^ odd) + j]
    previous = [ref.at[py] for ref in (spec0_ref, spec1_ref) for py in range(4)]
    for unit in range(8):
        first = 2 * ((unit // 4) ^ odd)
        for section, result in ((0, previous[unit]), (1, current.at[unit])):
            pixels = jnp.concatenate([patches_ref[section, unit % 4, first], patches_ref[section, unit % 4, first + 1]], axis=1)
            result[...] = spectrum(pixels, *forward)
    for unit in range(8):
        along_y, power = moments(previous[unit][...], current[unit], *inverse)
        sums_y[unit] = along_y
        sums_x[unit] = power

    flows = jnp.zeros((8, N), F32)
    for half in range(2):
        flows += placed_flows([sums_y[half * 4 + i] for i in range(4)], [sums_x[half * 4 + i] for i in range(4)], 1, 2 * (half ^ odd))
    flows_ref[...] = flows


def pack_nodes(out_ref, start_ref, weight_ref, edges_ref, nodes_ref, share_ref):
    out_ref[8:, :] = jnp.zeros((64, N), F32)
    fields = [start_ref[s, c] for s in range(2) for c in range(2)]
    fields += [weight_ref[0], weight_ref[1], edges_ref[0].astype(F32), edges_ref[2].astype(F32)]
    fields += [nodes_ref[k].astype(F32) for k in range(4)] + [share_ref[k] for k in range(4)]
    for at, field in enumerate(fields):
        row, lane = 8 + at // 4 * 16, at % 4 * GROUP + EDGE
        out_ref[row : row + 16, lane : lane + 16] = field


def chained_kernel(half, flags_ref, prior_ref, recv_ref, spec_ref, before_ref, table_ref, *rest):
    *node_refs, out_ref, previous = rest
    at_start, odd = flags_ref[0] == 0, flags_ref[1]
    forward = [table_ref[i] for i in range(3)]
    inverse = [table_ref[i] for i in range(3, 6)]
    first = 2 * (half ^ odd)
    if half == 0:
        pack_nodes(out_ref, *node_refs)
    else:
        out_ref[8:, :] = before_ref[8:, :]
    for py in range(4):
        own = jnp.concatenate([prior_ref[py, first], prior_ref[py, first + 1]], axis=1)
        other = jnp.concatenate([recv_ref[py, 0], recv_ref[py, 1]], axis=1)
        previous[py] = spectrum(jnp.where(at_start, own, other), *forward)
    sums = [moments(previous[py], spec_ref[py], *inverse) for py in range(4)]
    flows = before_ref[0:8, :] + placed_flows([s[0] for s in sums], [s[1] for s in sums], 0, first)
    out_ref[0:8, :] = flows


def beside(base, values, on_right):
    lane = lax.broadcasted_iota(jnp.int32, (8, N), 1) % 8
    left = jnp.where(lane < 2, pltpu.roll(values[:8], N - 4, 1), base[:8])
    right = jnp.where(lane >= 6, pltpu.roll(values[:8], 4, 1), base[:8])
    flows = jnp.where(on_right, right, left)
    lane = lax.broadcasted_iota(jnp.int32, (64, N), 1) % GROUP
    left = jnp.where(lane < EDGE, pltpu.roll(values[8:], N - 16, 1), base[8:])
    right = jnp.where((lane >= EDGE + 16) & (lane < 2 * EDGE + 16), pltpu.roll(values[8:], 16, 1), base[8:])
    return flows, jnp.where(on_right, right, left)


def far_columns_kernel(flags_ref, far_ref, own_ref, out_ref, field_ref):
    base = own_ref[...]
    flows, nodes = beside(base, far_ref[...] * flags_ref[2].astype(F32), flags_ref[1] == 1)
    out_ref[0:8, :] = flows
    out_ref[8:, :] = nodes
    for s in range(2):
        for c in range(2):
            lane = s * 16 + c * 8 + 2
            field_ref[s, c] = own_ref[2:6, lane : lane + 4]


def near_columns_kernel(flags_ref, partial_ref, near_ref, to_near_ref, to_far_ref):
    flows, nodes = beside(partial_ref[...], near_ref[...], flags_ref[1] == 0)
    top = jnp.concatenate([flows] + [nodes[16 * f : 16 * f + 8] for f in range(4)], axis=0)
    bottom = jnp.concatenate([flows] + [nodes[16 * f + 8 : 16 * f + 16] for f in range(4)], axis=0)
    odd = flags_ref[3] == 1
    to_near_ref[...] = jnp.where(odd, top, bottom)
    to_far_ref[...] = jnp.where(odd, bottom, top)


def shifted_rows(values, by):
    return pltpu.roll(values, by % values.shape[0], 0)


def nodes_kernel(flags_ref, to_near_ref, to_far_ref, near_ref, far_ref, spread_ref, out_ref):
    odd = flags_ref[3] == 1
    near, far = near_ref[...], far_ref[...] * flags_ref[4].astype(F32)
    above, below = jnp.where(odd, near, far), jnp.where(odd, far, near)
    top = jnp.where(odd, to_near_ref[...], to_far_ref[...])
    bottom = jnp.where(odd, to_far_ref[...], to_near_ref[...])

    row = lax.broadcasted_iota(jnp.int32, (8, N), 0)
    window = jnp.where(row < 2, pltpu.roll(above[:8], 4, 0), jnp.where(row < 6, top[:8], pltpu.roll(below[:8], 4, 0)))

    def field(at):
        part = slice(8 + 8 * at, 16 + 8 * at)
        return jnp.concatenate([above[part], top[part], bottom[part], below[part]], axis=0)

    moved, mixed, patch, share = (field(at) for at in range(4))

    narrow = window[:, : 4 * 8]
    part1 = narrow.astype(BF16)
    rest = narrow - part1.astype(F32)
    part2 = rest.astype(BF16)
    part3 = (rest - part2.astype(F32)).astype(BF16)
    spread = dot(jnp.concatenate([part1, part2, part3], axis=1), spread_ref[...])
    upper = row < 4
    lines = [[jnp.broadcast_to(spread[r : r + 1, b * N : (b + 1) * N], (8, N)) for b in range(3)] for r in range(8)]

    def patch_row(r):
        return lines[min(max(r, 0), 7)]

    rows4 = lax.broadcasted_iota(jnp.int32, (32, N), 0)
    lanes4 = lax.broadcasted_iota(jnp.int32, (32, N), 1)
    base = (1 + (rows4 + 8) % 16 // 4) * 6 + 1 + (lanes4 % GROUP + 16 - EDGE) % 16 // 4
    step = patch - base.astype(F32)

    def over_groups(values):
        values = values + pltpu.roll(values, GROUP, 1)
        return values + pltpu.roll(values, 2 * GROUP, 1)

    target = jnp.zeros((32, N), F32)
    for a in range(-1, 2):
        for b in range(-1, 2):
            weight = over_groups(jnp.where(step == float(6 * a + b), share, 0.0))
            moving = jnp.concatenate([jnp.where(upper, patch_row(2 * t + a)[b + 1], patch_row(2 * t + 1 + a)[b + 1]) for t in range(4)], axis=0)
            target = target + weight * moving

    group = lanes4 // GROUP
    stiff_pair = jnp.where(group < 2, mixed, 0.0)
    only0 = jnp.where(group == 0, mixed, 0.0)
    only1 = jnp.where(group == 1, mixed, 0.0)
    stiffness = only0 + pltpu.roll(only0, GROUP, 1) + pltpu.roll(only1, GROUP, 1) + pltpu.roll(only1, 2 * GROUP, 1)
    right = over_groups(jnp.where(group == 2, mixed, 0.0))
    down = over_groups(jnp.where(group == 3, mixed, 0.0))
    left = pltpu.roll(right, 1, 1)
    up = shifted_rows(down, 1)
    for _ in range(STEPS):
        springs = right * (pltpu.roll(moved, N - 1, 1) - moved) + left * (pltpu.roll(moved, 1, 1) - moved)
        springs = springs + down * (shifted_rows(moved, -1) - moved) + up * (shifted_rows(moved, 1) - moved)
        moved = moved + STEP_SIZE * (stiffness * (target - moved) + springs)
    for s in range(2):
        for c in range(2):
            lane = (2 * s + c) * GROUP + EDGE
            out_ref[s, c] = moved[8:24, lane : lane + 16]


@functools.lru_cache(maxsize=None)
def spread_table():
    table = np.zeros((3, 32, 3 * N))
    for b in range(3):
        for lane in range(N):
            group, node = lane // GROUP, lane % GROUP - EDGE
            col = node // 4 + 2 + b - 1
            if 0 <= col < 8 and node < 19:
                table[:, group * 8 + col, b * N + lane] = 1.0
    return table.reshape(96, 3 * N).astype(ml_dtypes.bfloat16)


def call(kernel, inputs, out_shapes, scratch=(), flops=0, moved=0):
    memory = [pltpu.SMEM] + [pltpu.VMEM] * (len(inputs) - 1)
    return pl.pallas_call(
        kernel,
        out_shape=out_shapes,
        in_specs=[pl.BlockSpec(memory_space=m) for m in memory],
        out_specs=jax.tree.map(lambda _: pl.BlockSpec(memory_space=pltpu.VMEM), out_shapes),
        scratch_shapes=scratch,
        compiler_params=pltpu.CompilerParams(vmem_limit_bytes=VMEM_LIMIT),
        cost_estimate=pl.CostEstimate(flops=flops, bytes_accessed=moved, transcendentals=0),
    )(*inputs)


def f32(*shape):
    return jax.ShapeDtypeStruct(shape, F32)


def near_partner(count):
    return [(i, i ^ 1) for i in range(count)]


def far_partner(count):
    pairs = []
    for i in range(count):
        other = i + 1 if i % 2 else i - 1
        pairs.append((i, other if 0 <= other < count else i))
    return pairs


def body(patches, prior_patches, node_patch, node_weight, edges, flow_weight, start_offset):
    gz, gy, gx = (lax.axis_index(a) for a in ("gz", "gy", "gx"))
    rows, cols = lax.axis_size("gy"), lax.axis_size("gx")
    odd, odd_row = gx % 2, gy % 2
    has_far = (gx > 0) & (gx < cols - 1)
    has_far_row = (gy > 0) & (gy < rows - 1)
    flags = jnp.stack([gz, odd, has_far, odd_row, has_far_row]).astype(jnp.int32)

    def to_next_section(values):
        return lax.ppermute(values, "gz", [(0, 1)])

    early = to_next_section(lax.dynamic_slice_in_dim(patches[1], 2 * odd, 2, axis=1))
    table = jnp.asarray(tables())
    half_spec = f32(4, N, 2 * N)
    spec0, spec1, flows, later = call(
        local_kernel,
        [flags, patches, table],
        [half_spec, half_spec, f32(8, N), jax.ShapeDtypeStruct((4, 2, N, N), BF16)],
        [pltpu.VMEM((8, N, 2 * N), F32), pltpu.VMEM((8, 1, N), F32), pltpu.VMEM((8, 1, 2 * N), F32)],
        flops=5_000_000_000, moved=4_000_000,
    )
    late = to_next_section(later)
    scratch = [pltpu.VMEM((4, N, 2 * N), F32)]
    (first,) = call(
        functools.partial(chained_kernel, 0),
        [flags, prior_patches, early, spec0, flows, table, start_offset, flow_weight, edges, node_patch, node_weight],
        [f32(72, N)], scratch, flops=2_000_000_000, moved=2_000_000,
    )
    from_far = lax.ppermute(first, "gx", far_partner(cols))
    (own,) = call(
        functools.partial(chained_kernel, 1), [flags, prior_patches, late, spec1, first, table],
        [f32(72, N)], scratch, flops=2_000_000_000, moved=2_000_000,
    )
    partial, flow_field = call(
        far_columns_kernel, [flags, from_far, own], [f32(72, N), f32(2, 2, 4, 4)], flops=5_000_000_000, moved=2_000_000)
    from_near = lax.ppermute(own, "gx", near_partner(cols))
    to_near, to_far = call(near_columns_kernel, [flags, partial, from_near], [f32(40, N), f32(40, N)])
    row_near = lax.ppermute(to_near, "gy", near_partner(rows))
    row_far = lax.ppermute(to_far, "gy", far_partner(rows))
    displacement = call(
        nodes_kernel, [flags, to_near, to_far, row_near, row_far, jnp.asarray(spread_table())], f32(2, 2, 16, 16))
    return flow_field, displacement


def solution(mesh):
    return jax.shard_map(
        body,
        mesh=mesh,
        in_specs=(
            P("gz", "gy", "gx", None, None),
            P("gy", "gx", None, None),
            P(None, "gy", "gx"),
            P(None, "gy", "gx"),
            P(None, "gy", "gx"),
            P("gz", "gy", "gx"),
            P("gz", None, "gy", "gx"),
        ),
        out_specs=(P("gz", None, "gy", "gx"), P("gz", None, "gy", "gx")),
        check_vma=False,
    )
```

```python
import functools
import math

import jax
import jax.numpy as jnp
import ml_dtypes
import numpy as np
from jax import lax
from jax.experimental import pallas as pl
from jax.experimental.pallas import tpu as pltpu
from jax.sharding import PartitionSpec as P

STEPS = 3
STEP_SIZE = 0.35
N = 128
H = N // 2
F32 = jnp.float32
BF16 = jnp.bfloat16
GROUP = 32
EDGE = 3
VMEM_LIMIT = 24 * 1024 * 1024


def split_const(values):
    high = values.astype(ml_dtypes.bfloat16)
    low = (values - high.astype(np.float64)).astype(ml_dtypes.bfloat16)
    return high, low


@functools.lru_cache(maxsize=None)
def tables():
    pixel = np.arange(N)
    phase = 2.0 * np.pi / N * (np.outer(np.arange(H), pixel) % N)
    cosine, sine = np.cos(phase), np.sin(phase)
    sine[0] = np.cos(np.pi * pixel)
    norm = np.full(H, math.sqrt(2.0 / N))
    norm[0] = math.sqrt(1.0 / N)
    basis = np.concatenate([cosine * norm[:, None], sine * norm[:, None]])
    root = basis / np.sqrt(np.concatenate([norm, norm]))[:, None]
    wide = np.zeros((2 * N, 2 * N))
    wide[:N, 0:H], wide[:N, N : N + H] = root[:H].T, root[H:].T
    wide[N:, H:N], wide[N:, N + H :] = root[:H].T, root[H:].T
    back = np.zeros((2 * N, 2 * N))
    back[0:H, :N], back[N : N + H, :N] = basis[:H], basis[H:]
    back[H:N, N:], back[N + H :, N:] = basis[:H], basis[H:]
    offset = ((pixel + H) % N - H).astype(np.float64)
    moment = (basis * offset[None, :]) @ basis.T
    stacked = []
    for left in (root, moment):
        high, low = split_const(left)
        stacked.append(np.block([[high, high], [low, low]]))
    return np.stack([*split_const(wide), stacked[0], stacked[1], *split_const(back)])


def dot(left, right):
    return jnp.dot(left, right, preferred_element_type=F32)


def halves(values):
    high = values.astype(BF16)
    return high, (values - high.astype(F32)).astype(BF16)


def left_product(stacked, values):
    high, low = halves(values)
    both = dot(stacked, jnp.concatenate([high, low], axis=0))
    return both[:N] + both[N:]


def spectrum(pixels, wide_high, wide_low, rows):
    return left_product(rows, dot(pixels, wide_high) + dot(pixels, wide_low))


def cross(prev, cur):
    lane = lax.broadcasted_iota(jnp.int32, (H, N), 1) % H == 0

    def part(start, stop, first_row):
        def quarter(whole, row, col):
            return whole[row + start : row + stop, col : col + N]

        pcc, pcs, psc, pss = (quarter(prev, r, c) for r in (0, H) for c in (0, N))
        qcc, qcs, qsc, qss = (quarter(cur, r, c) for r in (0, H) for c in (0, N))
        edge = lane[start:stop]
        u1, u2, u3, u4 = pcc * qcc, pss * qss, pcs * qcs, psc * qsc
        v1, v2, v3, v4 = pcc * qcs, pss * qsc, pcs * qcc, psc * qss
        w1, w2, w3, w4 = pcc * qsc, pss * qcs, pcs * qss, psc * qcc
        z = pcc * qss + pss * qcc - pcs * qsc - psc * qcs
        even, odd = u2 + u3, w3 - w2
        cc = u1 + u4 + jnp.where(edge, 0.0, even)
        cs = jnp.where(edge, even, (v1 - v3) + (v4 - v2))
        sc = (w1 - w4) + jnp.where(edge, 0.0, odd)
        ss = jnp.where(edge, odd, z)
        if first_row:
            top = lax.broadcasted_iota(jnp.int32, (stop - start, N), 0) == 0
            cc = jnp.where(top, u1 + jnp.where(edge, 0.0, u3), cc)
            cs = jnp.where(top, jnp.where(edge, u3, v1 - v3), cs)
            sc = jnp.where(top, u4 + jnp.where(edge, 0.0, u2), sc)
            ss = jnp.where(top, jnp.where(edge, u2, v4 - v2), ss)
        return jnp.concatenate([cc, cs], axis=1), jnp.concatenate([sc, ss], axis=1)

    first, rest = part(0, 8, True), part(8, H, False)
    return jnp.concatenate([first[0], rest[0], first[1], rest[1]], axis=0)


def moments(prev, cur, moment, back_high, back_low):
    values = cross(prev, cur)
    along_y = jnp.sum(values * left_product(moment, values), axis=0, keepdims=True)
    along_y = along_y[:, :N] + along_y[:, N:]
    high, low = halves(values)
    pixels = dot(high, back_high) + dot(low, back_high) + dot(high, back_low)
    return along_y, jnp.sum(pixels * pixels, axis=0, keepdims=True)


def placed_flows(along_y, power, section, first_col):
    lane = lax.broadcasted_iota(jnp.int32, (8, N), 1)
    offset = ((lane + H) % N - H).astype(F32)
    pad = jnp.zeros((2, N), F32)
    flows = jnp.zeros((8, N), F32)
    stacked_y = jnp.concatenate([pad, *along_y, pad], axis=0)
    for side in range(2):
        columns = jnp.concatenate([pad, *[p[:, side * N : (side + 1) * N] for p in power], pad], axis=0)
        energy = jnp.sum(columns, axis=1, keepdims=True) * (1.0 / (N * N)) + 1e-6
        mine = (lane < H) if side == 0 else (lane >= H)
        flow_y = jnp.sum(jnp.where(mine, stacked_y, 0.0), axis=1, keepdims=True) * (1.0 / (N * N)) / energy
        flow_x = jnp.sum(columns * offset, axis=1, keepdims=True) * (1.0 / (N * N)) / energy
        slot = section * 16 + 2 + first_col + side
        flows = jnp.where(lane == slot, flow_y, flows)
        flows = jnp.where(lane == slot + 8, flow_x, flows)
    return flows


def column_flows(sums_y, sums_x, first_unit, section, first_col):
    units = range(first_unit, first_unit + 4)
    return placed_flows([sums_y[u] for u in units], [sums_x[u] for u in units], section, first_col)


def group_lanes(rows):
    return lax.broadcasted_iota(jnp.int32, (rows, N), 1) % GROUP


def edge_columns(nodes, on_right):
    lane = group_lanes(16)
    edge = jnp.zeros((16, N), F32)
    for at in range(4):
        field, to = nodes[16 * at : 16 * at + 16], EDGE * at
        side = jnp.where(on_right, pltpu.roll(field, (to - 16) % N, 1), pltpu.roll(field, (to - EDGE) % N, 1))
        edge = jnp.where((lane >= to) & (lane < to + EDGE), side, edge)
    return edge


def beside(flows, nodes, message, on_right):
    lane = lax.broadcasted_iota(jnp.int32, (8, N), 1) % 8
    left = jnp.where(lane < 2, pltpu.roll(message[:8], N - 4, 1), flows)
    right = jnp.where(lane >= 6, pltpu.roll(message[:8], 4, 1), flows)
    lane, edge = group_lanes(16), message[8:]
    first = jnp.where(on_right, EDGE + 16, 0)
    place = (lane >= first) & (lane < first + EDGE)
    fields = []
    for at in range(4):
        side = jnp.where(on_right, pltpu.roll(edge, (EDGE + 16 - EDGE * at) % N, 1), pltpu.roll(edge, -EDGE * at % N, 1))
        fields.append(jnp.where(place, side, nodes[16 * at : 16 * at + 16]))
    return jnp.where(on_right, right, left), jnp.concatenate(fields, axis=0)


def own_kernel(flags_ref, flows_ref, middle_ref, edge_ref, out_ref):
    out_ref[0:8, :] = flows_ref[0:8, :] + middle_ref[...] * flags_ref[0].astype(F32)
    out_ref[8:, :] = edge_ref[...]


def far_columns_kernel(flags_ref, own_ref, nodes_ref, far_ref, out_ref):
    flows, nodes = beside(own_ref[0:8, :], nodes_ref[...], far_ref[...] * flags_ref[2].astype(F32), flags_ref[1] == 1)
    out_ref[0:8, :] = flows
    out_ref[8:, :] = nodes


def near_columns_kernel(flags_ref, partial_ref, near_ref, to_near_ref, to_far_ref):
    flows, nodes = beside(partial_ref[0:8, :], partial_ref[8:, :], near_ref[...], flags_ref[1] == 0)
    top = jnp.concatenate([flows] + [nodes[16 * f : 16 * f + 8] for f in range(4)], axis=0)
    bottom = jnp.concatenate([flows] + [nodes[16 * f + 8 : 16 * f + 16] for f in range(4)], axis=0)
    odd = flags_ref[3] == 1
    to_near_ref[...] = jnp.where(odd, top, bottom)
    to_far_ref[...] = jnp.where(odd, bottom, top)


def local_kernel(flags_ref, table_hbm, patches_hbm, prior_hbm, start_hbm, weight_hbm, edges_hbm, nodes_hbm, share_hbm,
                 spec_ref, flows_ref, field_ref, far_edge_ref, near_edge_ref, table_ref, patches_ref, prior_ref, start_ref, weight_ref, edges_ref, nodes_ref, share_ref,
                 before, sums_y, sums_x, sems):
    at_start, odd = flags_ref[0] == 0, flags_ref[1]
    pairs = [(table_hbm, table_ref), (patches_hbm, patches_ref), (prior_hbm, prior_ref), (start_hbm, start_ref),
             (weight_hbm, weight_ref), (edges_hbm, edges_ref), (nodes_hbm, nodes_ref), (share_hbm, share_ref)]
    copies = [pltpu.make_async_copy(source, target, sems.at[i]) for i, (source, target) in enumerate(pairs)]
    for copy in copies:
        copy.start()
    field_ref[...] = jnp.zeros((64, N), F32)
    for copy in copies[:2]:
        copy.wait()
    forward = [table_ref[i] for i in range(3)]
    inverse = [table_ref[i] for i in range(3, 6)]
    units = [(half, py) for half in range(2) for py in range(4)]

    def pixels(ref, index, first):
        return jnp.concatenate([ref[(*index, first)], ref[(*index, first + 1)]], axis=1)

    for half, py in units:
        for section in range(2):
            spec_ref[2 * section + half, py] = spectrum(pixels(patches_ref, (section, py), 2 * (half ^ odd)), *forward)
    for copy in copies[2:]:
        copy.wait()
    for unit, (half, py) in enumerate(units):
        before[unit] = spectrum(pixels(prior_ref, (py,), 2 * (half ^ odd)), *forward)
    for unit, (half, py) in enumerate(units):
        chain = [before[unit], spec_ref[half, py], spec_ref[2 + half, py]]
        for section in range(2):
            along_y, power = moments(chain[section], chain[section + 1], *inverse)
            sums_y[8 * section + unit] = along_y
            sums_x[8 * section + unit] = power

    flows = [sum(column_flows(sums_y, sums_x, 8 * s + 4 * half, s, 2 * (half ^ odd)) for half in range(2)) for s in range(2)]
    flows_ref[...] = jnp.where(at_start, flows[0], 0.0) + flows[1]

    fields = [start_ref[s, c] for s in range(2) for c in range(2)]
    fields += [weight_ref[0], weight_ref[1], edges_ref[0].astype(F32), edges_ref[2].astype(F32)]
    fields += [nodes_ref[k].astype(F32) for k in range(4)] + [share_ref[k] for k in range(4)]
    for at, field in enumerate(fields):
        row, lane = at // 4 * 16, at % 4 * GROUP + EDGE
        field_ref[row : row + 16, lane : lane + 16] = field
    nodes = field_ref[...]
    far_edge_ref[...] = edge_columns(nodes, odd == 1)
    near_edge_ref[...] = edge_columns(nodes, odd == 0)


def middle_kernel(flags_ref, recv_ref, spec_ref, flows_ref, edge_ref, table_ref, out_ref, middle_ref, other, sums_y, sums_x):
    gz, odd = flags_ref[0], flags_ref[1]
    forward = [table_ref[i] for i in range(3)]
    inverse = [table_ref[i] for i in range(3, 6)]
    own = 3 * (1 - gz)
    for py in range(4):
        other[py] = spectrum(jnp.concatenate([recv_ref[py, 0], recv_ref[py, 1]], axis=1), *forward)
    for py in range(4):
        mine, theirs = spec_ref[own, py], other[py]
        prev, cur = jnp.where(gz == 0, mine, theirs), jnp.where(gz == 0, theirs, mine)
        sums_y[py], sums_x[py] = moments(prev, cur, *inverse)
    flows = column_flows(sums_y, sums_x, 0, 0, 2 * (1 - gz ^ odd))
    middle_ref[...] = flows
    out_ref[0:8, :] = flows_ref[...] + jnp.where(gz == 0, 0.0, flows)
    out_ref[8:, :] = edge_ref[...]


def shifted_rows(values, by):
    return pltpu.roll(values, by % values.shape[0], 0)


def nodes_kernel(flags_ref, to_near_ref, to_far_ref, far_ref, near_ref, spread_ref, field_ref, out_ref):
    odd = flags_ref[3] == 1
    near, far = near_ref[...], far_ref[...] * flags_ref[4].astype(F32)
    above, below = jnp.where(odd, near, far), jnp.where(odd, far, near)
    top = jnp.where(odd, to_near_ref[...], to_far_ref[...])
    bottom = jnp.where(odd, to_far_ref[...], to_near_ref[...])

    row = lax.broadcasted_iota(jnp.int32, (8, N), 0)
    window = jnp.where(row < 2, pltpu.roll(above[:8], 4, 0), jnp.where(row < 6, top[:8], pltpu.roll(below[:8], 4, 0)))

    def field(at):
        part = slice(8 + 8 * at, 16 + 8 * at)
        return jnp.concatenate([above[part], top[part], bottom[part], below[part]], axis=0)

    moved, mixed, patch, share = (field(at) for at in range(4))

    narrow = window[:, : 4 * 8]
    part1 = narrow.astype(BF16)
    rest = narrow - part1.astype(F32)
    part2 = rest.astype(BF16)
    part3 = (rest - part2.astype(F32)).astype(BF16)
    spread = dot(jnp.concatenate([part1, part2, part3], axis=1), spread_ref[...])
    upper = row < 4
    lines = [[jnp.broadcast_to(spread[r : r + 1, b * N : (b + 1) * N], (8, N)) for b in range(3)] for r in range(8)]

    def patch_row(r):
        return lines[min(max(r, 0), 7)]

    rows4 = lax.broadcasted_iota(jnp.int32, (32, N), 0)
    lanes4 = lax.broadcasted_iota(jnp.int32, (32, N), 1)
    base = (1 + (rows4 + 8) % 16 // 4) * 6 + 1 + (lanes4 % GROUP + 16 - EDGE) % 16 // 4
    step = patch - base.astype(F32)

    def over_groups(values):
        values = values + pltpu.roll(values, GROUP, 1)
        return values + pltpu.roll(values, 2 * GROUP, 1)

    target = jnp.zeros((32, N), F32)
    for a in range(-1, 2):
        for b in range(-1, 2):
            weight = over_groups(jnp.where(step == float(6 * a + b), share, 0.0))
            moving = jnp.concatenate([jnp.where(upper, patch_row(2 * t + a)[b + 1], patch_row(2 * t + 1 + a)[b + 1]) for t in range(4)], axis=0)
            target = target + weight * moving

    group = lanes4 // GROUP
    stiff_pair = jnp.where(group < 2, mixed, 0.0)
    only0 = jnp.where(group == 0, mixed, 0.0)
    only1 = jnp.where(group == 1, mixed, 0.0)
    stiffness = only0 + pltpu.roll(only0, GROUP, 1) + pltpu.roll(only1, GROUP, 1) + pltpu.roll(only1, 2 * GROUP, 1)
    right = over_groups(jnp.where(group == 2, mixed, 0.0))
    down = over_groups(jnp.where(group == 3, mixed, 0.0))
    left = pltpu.roll(right, 1, 1)
    up = shifted_rows(down, 1)
    for _ in range(STEPS):
        springs = right * (pltpu.roll(moved, N - 1, 1) - moved) + left * (pltpu.roll(moved, 1, 1) - moved)
        springs = springs + down * (shifted_rows(moved, -1) - moved) + up * (shifted_rows(moved, 1) - moved)
        moved = moved + STEP_SIZE * (stiffness * (target - moved) + springs)
    for s in range(2):
        for c in range(2):
            lane = s * 16 + c * 8 + 2
            field_ref[s, c] = top[2:6, lane : lane + 4]
            lane = (2 * s + c) * GROUP + EDGE
            out_ref[s, c] = moved[8:24, lane : lane + 16]


@functools.lru_cache(maxsize=None)
def spread_table():
    table = np.zeros((3, 32, 3 * N))
    for b in range(3):
        for lane in range(N):
            group, node = lane // GROUP, lane % GROUP - EDGE
            col = node // 4 + 2 + b - 1
            if 0 <= col < 8 and node < 19:
                table[:, group * 8 + col, b * N + lane] = 1.0
    return table.reshape(96, 3 * N).astype(ml_dtypes.bfloat16)


def call(kernel, inputs, out_shapes, scratch=(), flops=0, moved=0, from_hbm=()):
    from_hbm = [pltpu.with_memory_space_constraint(a, pltpu.HBM) for a in from_hbm]
    memory = [pltpu.SMEM] + [pltpu.VMEM] * (len(inputs) - 1) + [pltpu.HBM] * len(from_hbm)
    return pl.pallas_call(
        kernel,
        out_shape=out_shapes,
        in_specs=[pl.BlockSpec(memory_space=m) for m in memory],
        out_specs=jax.tree.map(lambda _: pl.BlockSpec(memory_space=pltpu.VMEM), out_shapes),
        scratch_shapes=scratch,
        compiler_params=pltpu.CompilerParams(vmem_limit_bytes=VMEM_LIMIT),
        cost_estimate=pl.CostEstimate(flops=flops, bytes_accessed=moved, transcendentals=0),
    )(*inputs, *from_hbm)


def f32(*shape):
    return jax.ShapeDtypeStruct(shape, F32)


def near_partner(count):
    return [(i, i ^ 1) for i in range(count)]


def far_partner(count):
    pairs = []
    for i in range(count):
        other = i + 1 if i % 2 else i - 1
        pairs.append((i, other if 0 <= other < count else i))
    return pairs


def body(patches, prior_patches, node_patch, node_weight, edges, flow_weight, start_offset):
    gz, gy, gx = (lax.axis_index(a) for a in ("gz", "gy", "gx"))
    rows, cols = lax.axis_size("gy"), lax.axis_size("gx")
    odd, odd_row = gx % 2, gy % 2
    has_far = (gx > 0) & (gx < cols - 1)
    has_far_row = (gy > 0) & (gy < rows - 1)
    flags = jnp.stack([gz, odd, has_far, odd_row, has_far_row]).astype(jnp.int32)
    table = jnp.asarray(tables())

    first_col = 2 * (odd ^ gz)
    chunk = lax.dynamic_slice(patches, (1 - gz, 0, first_col, 0, 0), (1, 4, 2, N, N))[0]
    received = lax.ppermute(chunk, "gz", [(0, 1), (1, 0)])
    sums = [pltpu.VMEM((16, 1, N), F32), pltpu.VMEM((16, 1, 2 * N), F32)]
    arrays = [patches, prior_patches, start_offset, flow_weight, edges, node_patch, node_weight]
    spec, flows, nodes, far_edge, near_edge, table = call(
        local_kernel, [flags],
        [f32(4, 4, N, 2 * N), f32(8, N), f32(64, N), f32(16, N), f32(16, N), jax.ShapeDtypeStruct(table.shape, table.dtype)],
        [*(pltpu.VMEM(a.shape, a.dtype) for a in arrays), pltpu.VMEM((8, N, 2 * N), F32), *sums, pltpu.SemaphoreType.DMA((8,))],
        flops=8_000_000_000, moved=4_000_000, from_hbm=[table, *arrays],
    )
    to_far, middle = call(
        middle_kernel, [flags, received, spec, flows, far_edge, table],
        [f32(24, N), f32(8, N)], [pltpu.VMEM((4, N, 2 * N), F32), *sums],
        flops=2_000_000_000, moved=2_000_000,
    )
    own_middle = lax.ppermute(middle, "gz", [(0, 1), (1, 0)])
    from_far = lax.ppermute(to_far, "gx", far_partner(cols))
    to_near = call(own_kernel, [flags, to_far, own_middle, near_edge], f32(24, N), flops=1_000_000_000, moved=1_000_000)
    from_near = lax.ppermute(to_near, "gx", near_partner(cols))
    partial = call(far_columns_kernel, [flags, to_near, nodes, from_far], f32(72, N), flops=5_000_000_000, moved=2_000_000)
    to_near, to_far = call(near_columns_kernel, [flags, partial, from_near], [f32(40, N), f32(40, N)])
    row_far = lax.ppermute(to_far, "gy", far_partner(rows))
    row_near = lax.ppermute(to_near, "gy", near_partner(rows))
    flow_field, displacement = call(
        nodes_kernel, [flags, to_near, to_far, row_far, row_near, jnp.asarray(spread_table())],
        [f32(2, 2, 4, 4), f32(2, 2, 16, 16)])
    return flow_field, displacement


def solution(mesh):
    return jax.shard_map(
        body,
        mesh=mesh,
        in_specs=(
            P("gz", "gy", "gx", None, None),
            P("gy", "gx", None, None),
            P(None, "gy", "gx"),
            P(None, "gy", "gx"),
            P(None, "gy", "gx"),
            P("gz", "gy", "gx"),
            P("gz", None, "gy", "gx"),
        ),
        out_specs=(P("gz", None, "gy", "gx"), P("gz", None, "gy", "gx")),
        check_vma=False,
    )
```

```python
import functools
import math

import jax
import jax.numpy as jnp
import ml_dtypes
import numpy as np
from jax import lax
from jax.experimental import pallas as pl
from jax.experimental.pallas import tpu as pltpu
from jax.sharding import PartitionSpec as P

STEPS = 3
STEP_SIZE = 0.35
N = 128
H = N // 2
F32 = jnp.float32
BF16 = jnp.bfloat16
GROUP = 32
EDGE = 3
VMEM_LIMIT = 24 * 1024 * 1024


def split_const(values):
    high = values.astype(ml_dtypes.bfloat16)
    low = (values - high.astype(np.float64)).astype(ml_dtypes.bfloat16)
    return high, low


@functools.lru_cache(maxsize=None)
def tables():
    pixel = np.arange(N)
    phase = 2.0 * np.pi / N * (np.outer(np.arange(H), pixel) % N)
    cosine, sine = np.cos(phase), np.sin(phase)
    sine[0] = np.cos(np.pi * pixel)
    norm = np.full(H, math.sqrt(2.0 / N))
    norm[0] = math.sqrt(1.0 / N)
    basis = np.concatenate([cosine * norm[:, None], sine * norm[:, None]])
    root = basis / np.sqrt(np.concatenate([norm, norm]))[:, None]
    wide = np.zeros((2 * N, 2 * N))
    wide[:N, 0:H], wide[:N, N : N + H] = root[:H].T, root[H:].T
    wide[N:, H:N], wide[N:, N + H :] = root[:H].T, root[H:].T
    back = np.zeros((2 * N, 2 * N))
    back[0:H, :N], back[N : N + H, :N] = basis[:H], basis[H:]
    back[H:N, N:], back[N + H :, N:] = basis[:H], basis[H:]
    offset = ((pixel + H) % N - H).astype(np.float64)
    moment = (basis * offset[None, :]) @ basis.T
    stacked = []
    for left in (root, moment):
        high, low = split_const(left)
        stacked.append(np.block([[high, high], [low, low]]))
    return np.stack([*split_const(wide), stacked[0], stacked[1], *split_const(back)])


def dot(left, right):
    return jnp.dot(left, right, preferred_element_type=F32)


def halves(values):
    high = values.astype(BF16)
    return high, (values - high.astype(F32)).astype(BF16)


def left_product(stacked, values):
    high, low = halves(values)
    both = dot(stacked, jnp.concatenate([high, low], axis=0))
    return both[:N] + both[N:]


def spectrum(pixels, wide_high, wide_low, rows):
    return left_product(rows, dot(pixels, wide_high) + dot(pixels, wide_low))


def cross(prev, cur):
    lane = lax.broadcasted_iota(jnp.int32, (H, N), 1) % H == 0

    def part(start, stop, first_row):
        def quarter(whole, row, col):
            return whole[row + start : row + stop, col : col + N]

        pcc, pcs, psc, pss = (quarter(prev, r, c) for r in (0, H) for c in (0, N))
        qcc, qcs, qsc, qss = (quarter(cur, r, c) for r in (0, H) for c in (0, N))
        edge = lane[start:stop]
        u1, u2, u3, u4 = pcc * qcc, pss * qss, pcs * qcs, psc * qsc
        v1, v2, v3, v4 = pcc * qcs, pss * qsc, pcs * qcc, psc * qss
        w1, w2, w3, w4 = pcc * qsc, pss * qcs, pcs * qss, psc * qcc
        z = pcc * qss + pss * qcc - pcs * qsc - psc * qcs
        even, odd = u2 + u3, w3 - w2
        cc = u1 + u4 + jnp.where(edge, 0.0, even)
        cs = jnp.where(edge, even, (v1 - v3) + (v4 - v2))
        sc = (w1 - w4) + jnp.where(edge, 0.0, odd)
        ss = jnp.where(edge, odd, z)
        if first_row:
            top = lax.broadcasted_iota(jnp.int32, (stop - start, N), 0) == 0
            cc = jnp.where(top, u1 + jnp.where(edge, 0.0, u3), cc)
            cs = jnp.where(top, jnp.where(edge, u3, v1 - v3), cs)
            sc = jnp.where(top, u4 + jnp.where(edge, 0.0, u2), sc)
            ss = jnp.where(top, jnp.where(edge, u2, v4 - v2), ss)
        return jnp.concatenate([cc, cs], axis=1), jnp.concatenate([sc, ss], axis=1)

    first, rest = part(0, 8, True), part(8, H, False)
    return jnp.concatenate([first[0], rest[0], first[1], rest[1]], axis=0)


def moments(prev, cur, moment, back_high, back_low):
    values = cross(prev, cur)
    along_y = jnp.sum(values * left_product(moment, values), axis=0, keepdims=True)
    along_y = along_y[:, :N] + along_y[:, N:]
    high, low = halves(values)
    pixels = dot(high, back_high) + dot(low, back_high) + dot(high, back_low)
    return along_y, jnp.sum(pixels * pixels, axis=0, keepdims=True)


def placed_flows(along_y, power, section, first_col):
    lane = lax.broadcasted_iota(jnp.int32, (8, N), 1)
    offset = ((lane + H) % N - H).astype(F32)
    pad = jnp.zeros((2, N), F32)
    flows = jnp.zeros((8, N), F32)
    stacked_y = jnp.concatenate([pad, *along_y, pad], axis=0)
    for side in range(2):
        columns = jnp.concatenate([pad, *[p[:, side * N : (side + 1) * N] for p in power], pad], axis=0)
        energy = jnp.sum(columns, axis=1, keepdims=True) * (1.0 / (N * N)) + 1e-6
        mine = (lane < H) if side == 0 else (lane >= H)
        flow_y = jnp.sum(jnp.where(mine, stacked_y, 0.0), axis=1, keepdims=True) * (1.0 / (N * N)) / energy
        flow_x = jnp.sum(columns * offset, axis=1, keepdims=True) * (1.0 / (N * N)) / energy
        slot = section * 16 + 2 + first_col + side
        flows = jnp.where(lane == slot, flow_y, flows)
        flows = jnp.where(lane == slot + 8, flow_x, flows)
    return flows


def column_flows(sums_y, sums_x, first_unit, section, first_col):
    units = range(first_unit, first_unit + 4)
    return placed_flows([sums_y[u] for u in units], [sums_x[u] for u in units], section, first_col)


def group_lanes(rows):
    return lax.broadcasted_iota(jnp.int32, (rows, N), 1) % GROUP


def edge_columns(nodes, on_right):
    lane = group_lanes(16)
    edge = jnp.zeros((16, N), F32)
    for at in range(4):
        field, to = nodes[16 * at : 16 * at + 16], EDGE * at
        side = jnp.where(on_right, pltpu.roll(field, (to - 16) % N, 1), pltpu.roll(field, (to - EDGE) % N, 1))
        edge = jnp.where((lane >= to) & (lane < to + EDGE), side, edge)
    return edge


def beside(flows, nodes, message, on_right):
    lane = lax.broadcasted_iota(jnp.int32, (8, N), 1) % 8
    left = jnp.where(lane < 2, pltpu.roll(message[:8], N - 4, 1), flows)
    right = jnp.where(lane >= 6, pltpu.roll(message[:8], 4, 1), flows)
    lane, edge = group_lanes(16), message[8:]
    first = jnp.where(on_right, EDGE + 16, 0)
    place = (lane >= first) & (lane < first + EDGE)
    fields = []
    for at in range(4):
        side = jnp.where(on_right, pltpu.roll(edge, (EDGE + 16 - EDGE * at) % N, 1), pltpu.roll(edge, -EDGE * at % N, 1))
        fields.append(jnp.where(place, side, nodes[16 * at : 16 * at + 16]))
    return jnp.where(on_right, right, left), jnp.concatenate(fields, axis=0)


def far_columns_kernel(flags_ref, own_ref, nodes_ref, far_ref, out_ref):
    flows, nodes = beside(own_ref[...], nodes_ref[...], far_ref[...] * flags_ref[2].astype(F32), flags_ref[1] == 1)
    out_ref[0:8, :] = flows
    out_ref[8:, :] = nodes


def local_kernel(flags_ref, table_hbm, patches_hbm, prior_hbm, start_hbm, weight_hbm, edges_hbm, nodes_hbm, share_hbm,
                 spec_ref, flows_ref, field_ref, far_edge_ref, near_edge_ref, table_ref, patches_ref, prior_ref, start_ref, weight_ref, edges_ref, nodes_ref, share_ref,
                 before, sums_y, sums_x, sems):
    at_start, odd = flags_ref[0] == 0, flags_ref[1]
    pairs = [(table_hbm, table_ref), (patches_hbm, patches_ref), (prior_hbm, prior_ref), (start_hbm, start_ref),
             (weight_hbm, weight_ref), (edges_hbm, edges_ref), (nodes_hbm, nodes_ref), (share_hbm, share_ref)]
    copies = [pltpu.make_async_copy(source, target, sems.at[i]) for i, (source, target) in enumerate(pairs)]
    for copy in copies:
        copy.start()
    field_ref[...] = jnp.zeros((64, N), F32)
    for copy in copies[:2]:
        copy.wait()
    forward = [table_ref[i] for i in range(3)]
    inverse = [table_ref[i] for i in range(3, 6)]
    units = [(half, py) for half in range(2) for py in range(4)]

    def pixels(ref, index, first):
        return jnp.concatenate([ref[(*index, first)], ref[(*index, first + 1)]], axis=1)

    for half, py in units:
        for section in range(2):
            spec_ref[2 * section + half, py] = spectrum(pixels(patches_ref, (section, py), 2 * (half ^ odd)), *forward)
    for copy in copies[2:]:
        copy.wait()
    for unit, (half, py) in enumerate(units):
        before[unit] = spectrum(pixels(prior_ref, (py,), 2 * (half ^ odd)), *forward)
    for unit, (half, py) in enumerate(units):
        chain = [before[unit], spec_ref[half, py], spec_ref[2 + half, py]]
        for section in range(2):
            along_y, power = moments(chain[section], chain[section + 1], *inverse)
            sums_y[8 * section + unit] = along_y
            sums_x[8 * section + unit] = power

    flows = [sum(column_flows(sums_y, sums_x, 8 * s + 4 * half, s, 2 * (half ^ odd)) for half in range(2)) for s in range(2)]
    flows_ref[...] = jnp.where(at_start, flows[0], 0.0) + flows[1]

    fields = [start_ref[s, c] for s in range(2) for c in range(2)]
    fields += [weight_ref[0], weight_ref[1], edges_ref[0].astype(F32), edges_ref[2].astype(F32)]
    fields += [nodes_ref[k].astype(F32) for k in range(4)] + [share_ref[k] for k in range(4)]
    for at, field in enumerate(fields):
        row, lane = at // 4 * 16, at % 4 * GROUP + EDGE
        field_ref[row : row + 16, lane : lane + 16] = field
    nodes = field_ref[...]
    far_edge_ref[...] = edge_columns(nodes, odd == 1)
    near_edge_ref[...] = edge_columns(nodes, odd == 0)


def middle_kernel(flags_ref, recv_ref, spec_ref, flows_ref, edge_ref, table_ref, out_ref, middle_ref, other, sums_y, sums_x):
    gz, odd = flags_ref[0], flags_ref[1]
    forward = [table_ref[i] for i in range(3)]
    inverse = [table_ref[i] for i in range(3, 6)]
    own = 3 * (1 - gz)
    for py in range(4):
        other[py] = spectrum(jnp.concatenate([recv_ref[py, 0], recv_ref[py, 1]], axis=1), *forward)
    for py in range(4):
        mine, theirs = spec_ref[own, py], other[py]
        prev, cur = jnp.where(gz == 0, mine, theirs), jnp.where(gz == 0, theirs, mine)
        sums_y[py], sums_x[py] = moments(prev, cur, *inverse)
    flows = column_flows(sums_y, sums_x, 0, 0, 2 * (1 - gz ^ odd))
    middle_ref[...] = flows
    out_ref[0:8, :] = flows_ref[...] + jnp.where(gz == 0, 0.0, flows)
    out_ref[8:, :] = edge_ref[...]


def shifted_rows(values, by):
    return pltpu.roll(values, by % values.shape[0], 0)


def nodes_kernel(flags_ref, to_near_ref, to_far_ref, far_ref, near_ref, spread_ref, field_ref, out_ref):
    odd, near_on_right = flags_ref[3] == 1, flags_ref[1] == 0
    near, far = near_ref[...], far_ref[...]
    above, below = jnp.where(odd, near, far), jnp.where(odd, far, near)
    top = jnp.where(odd, to_near_ref[...], to_far_ref[...])
    bottom = jnp.where(odd, to_far_ref[...], to_near_ref[...])
    blocks = (above, top, bottom, below)
    flow_lane, lane = lax.broadcasted_iota(jnp.int32, (8, N), 1) % 8, group_lanes(8)
    flow_side = jnp.where(near_on_right, 6, 0)
    first = jnp.where(near_on_right, EDGE + 16, 0)

    def flows_of(block):
        side = jnp.where(near_on_right, pltpu.roll(block[8:16], 4, 1), pltpu.roll(block[8:16], N - 4, 1))
        return jnp.where((flow_lane >= flow_side) & (flow_lane < flow_side + 2), side, block[0:8])

    def field(at):
        rows = []
        for block in blocks:
            edge = block[48:56]
            side = jnp.where(near_on_right, pltpu.roll(edge, (EDGE + 16 - EDGE * at) % N, 1), pltpu.roll(edge, -EDGE * at % N, 1))
            rows.append(jnp.where((lane >= first) & (lane < first + EDGE), side, block[16 + 8 * at : 24 + 8 * at]))
        return jnp.concatenate(rows, axis=0)

    moved, mixed, patch, share = (field(at) for at in range(4))
    own_flows = flows_of(top)
    row = lax.broadcasted_iota(jnp.int32, (8, N), 0)
    window = jnp.where(row < 2, pltpu.roll(flows_of(above), 4, 0), jnp.where(row < 6, own_flows, pltpu.roll(flows_of(below), 4, 0)))

    narrow = window[:, : 4 * 8]
    part1 = narrow.astype(BF16)
    rest = narrow - part1.astype(F32)
    part2 = rest.astype(BF16)
    part3 = (rest - part2.astype(F32)).astype(BF16)
    spread = dot(jnp.concatenate([part1, part2, part3], axis=1), spread_ref[...])
    upper = row < 4
    lines = [[jnp.broadcast_to(spread[r : r + 1, b * N : (b + 1) * N], (8, N)) for b in range(3)] for r in range(8)]

    def patch_row(r):
        return lines[min(max(r, 0), 7)]

    rows4 = lax.broadcasted_iota(jnp.int32, (32, N), 0)
    lanes4 = lax.broadcasted_iota(jnp.int32, (32, N), 1)
    base = (1 + (rows4 + 8) % 16 // 4) * 6 + 1 + (lanes4 % GROUP + 16 - EDGE) % 16 // 4
    step = patch - base.astype(F32)

    def over_groups(values):
        values = values + pltpu.roll(values, GROUP, 1)
        return values + pltpu.roll(values, 2 * GROUP, 1)

    target = jnp.zeros((32, N), F32)
    for a in range(-1, 2):
        for b in range(-1, 2):
            weight = over_groups(jnp.where(step == float(6 * a + b), share, 0.0))
            moving = jnp.concatenate([jnp.where(upper, patch_row(2 * t + a)[b + 1], patch_row(2 * t + 1 + a)[b + 1]) for t in range(4)], axis=0)
            target = target + weight * moving

    group = lanes4 // GROUP
    stiff_pair = jnp.where(group < 2, mixed, 0.0)
    only0 = jnp.where(group == 0, mixed, 0.0)
    only1 = jnp.where(group == 1, mixed, 0.0)
    stiffness = only0 + pltpu.roll(only0, GROUP, 1) + pltpu.roll(only1, GROUP, 1) + pltpu.roll(only1, 2 * GROUP, 1)
    right = over_groups(jnp.where(group == 2, mixed, 0.0))
    down = over_groups(jnp.where(group == 3, mixed, 0.0))
    left = pltpu.roll(right, 1, 1)
    up = shifted_rows(down, 1)
    for _ in range(STEPS):
        springs = right * (pltpu.roll(moved, N - 1, 1) - moved) + left * (pltpu.roll(moved, 1, 1) - moved)
        springs = springs + down * (shifted_rows(moved, -1) - moved) + up * (shifted_rows(moved, 1) - moved)
        moved = moved + STEP_SIZE * (stiffness * (target - moved) + springs)
    for s in range(2):
        for c in range(2):
            lane = s * 16 + c * 8 + 2
            field_ref[s, c] = own_flows[2:6, lane : lane + 4]
            lane = (2 * s + c) * GROUP + EDGE
            out_ref[s, c] = moved[8:24, lane : lane + 16]


@functools.lru_cache(maxsize=None)
def spread_table():
    table = np.zeros((3, 32, 3 * N))
    for b in range(3):
        for lane in range(N):
            group, node = lane // GROUP, lane % GROUP - EDGE
            col = node // 4 + 2 + b - 1
            if 0 <= col < 8 and node < 19:
                table[:, group * 8 + col, b * N + lane] = 1.0
    return table.reshape(96, 3 * N).astype(ml_dtypes.bfloat16)


def call(kernel, inputs, out_shapes, scratch=(), flops=0, moved=0, from_hbm=()):
    from_hbm = [pltpu.with_memory_space_constraint(a, pltpu.HBM) for a in from_hbm]
    memory = [pltpu.SMEM] + [pltpu.VMEM] * (len(inputs) - 1) + [pltpu.HBM] * len(from_hbm)
    return pl.pallas_call(
        kernel,
        out_shape=out_shapes,
        in_specs=[pl.BlockSpec(memory_space=m) for m in memory],
        out_specs=jax.tree.map(lambda _: pl.BlockSpec(memory_space=pltpu.VMEM), out_shapes),
        scratch_shapes=scratch,
        compiler_params=pltpu.CompilerParams(vmem_limit_bytes=VMEM_LIMIT),
        cost_estimate=pl.CostEstimate(flops=flops, bytes_accessed=moved, transcendentals=0),
    )(*inputs, *from_hbm)


def f32(*shape):
    return jax.ShapeDtypeStruct(shape, F32)


def near_partner(count):
    return [(i, i ^ 1) for i in range(count)]


def far_partner(count):
    pairs = []
    for i in range(count):
        other = i + 1 if i % 2 else i - 1
        pairs.append((i, other if 0 <= other < count else i))
    return pairs


def body(patches, prior_patches, node_patch, node_weight, edges, flow_weight, start_offset):
    gz, gy, gx = (lax.axis_index(a) for a in ("gz", "gy", "gx"))
    rows, cols = lax.axis_size("gy"), lax.axis_size("gx")
    odd, odd_row = gx % 2, gy % 2
    has_far = (gx > 0) & (gx < cols - 1)
    has_far_row = (gy > 0) & (gy < rows - 1)
    flags = jnp.stack([gz, odd, has_far, odd_row]).astype(jnp.int32)
    table = jnp.asarray(tables())

    first_col = 2 * (odd ^ gz)
    chunk = lax.dynamic_slice(patches, (1 - gz, 0, first_col, 0, 0), (1, 4, 2, N, N))[0]
    received = lax.ppermute(chunk, "gz", [(0, 1), (1, 0)])
    sums = [pltpu.VMEM((16, 1, N), F32), pltpu.VMEM((16, 1, 2 * N), F32)]
    arrays = [patches, prior_patches, start_offset, flow_weight, edges, node_patch, node_weight]
    spec, flows, nodes, far_edge, near_edge, table = call(
        local_kernel, [flags],
        [f32(4, 4, N, 2 * N), f32(8, N), f32(64, N), f32(16, N), f32(16, N), jax.ShapeDtypeStruct(table.shape, table.dtype)],
        [*(pltpu.VMEM(a.shape, a.dtype) for a in arrays), pltpu.VMEM((8, N, 2 * N), F32), *sums, pltpu.SemaphoreType.DMA((8,))],
        flops=8_000_000_000, moved=4_000_000, from_hbm=[table, *arrays],
    )
    to_far, middle = call(
        middle_kernel, [flags, received, spec, flows, far_edge, table],
        [f32(24, N), f32(8, N)], [pltpu.VMEM((4, N, 2 * N), F32), *sums],
        flops=2_000_000_000, moved=2_000_000,
    )
    own_middle = lax.ppermute(middle, "gz", [(0, 1), (1, 0)])
    from_far = lax.ppermute(to_far, "gx", far_partner(cols))
    own = to_far[:8] + own_middle * gz.astype(F32)
    from_near = lax.ppermute(jnp.concatenate([own, near_edge]), "gx", near_partner(cols))
    partial = call(far_columns_kernel, [flags, own, nodes, from_far], f32(72, N), flops=5_000_000_000, moved=2_000_000)

    def rows_of(first):
        return jnp.concatenate([partial[:8], from_near[:8]] + [partial[8 + 16 * f + first :][:8] for f in range(4)] + [from_near[8 + first :][:8]])

    top, bottom = rows_of(0), rows_of(8)
    to_near, to_far = jnp.where(odd_row == 1, top, bottom), jnp.where(odd_row == 1, bottom, top)
    row_far = lax.ppermute(to_far, "gy", far_partner(rows)) * has_far_row.astype(F32)
    row_near = lax.ppermute(to_near, "gy", near_partner(rows))
    flow_field, displacement = call(
        nodes_kernel, [flags, to_near, to_far, row_far, row_near, jnp.asarray(spread_table())],
        [f32(2, 2, 4, 4), f32(2, 2, 16, 16)])
    return flow_field, displacement


def solution(mesh):
    return jax.shard_map(
        body,
        mesh=mesh,
        in_specs=(
            P("gz", "gy", "gx", None, None),
            P("gy", "gx", None, None),
            P(None, "gy", "gx"),
            P(None, "gy", "gx"),
            P(None, "gy", "gx"),
            P("gz", "gy", "gx"),
            P("gz", None, "gy", "gx"),
        ),
        out_specs=(P("gz", None, "gy", "gx"), P("gz", None, "gy", "gx")),
        check_vma=False,
    )
```

```python
import functools
import math

import jax
import jax.numpy as jnp
import ml_dtypes
import numpy as np
from jax import lax
from jax.experimental import pallas as pl
from jax.experimental.pallas import tpu as pltpu
from jax.sharding import PartitionSpec as P

STEPS = 3
STEP_SIZE = 0.35
N = 128
H = N // 2
F32 = jnp.float32
BF16 = jnp.bfloat16
GROUP = 32
EDGE = 3
VMEM_LIMIT = 24 * 1024 * 1024


def split_const(values):
    high = values.astype(ml_dtypes.bfloat16)
    low = (values - high.astype(np.float64)).astype(ml_dtypes.bfloat16)
    return high, low


@functools.lru_cache(maxsize=None)
def tables():
    pixel = np.arange(N)
    phase = 2.0 * np.pi / N * (np.outer(np.arange(H), pixel) % N)
    cosine, sine = np.cos(phase), np.sin(phase)
    sine[0] = np.cos(np.pi * pixel)
    norm = np.full(H, math.sqrt(2.0 / N))
    norm[0] = math.sqrt(1.0 / N)
    basis = np.concatenate([cosine * norm[:, None], sine * norm[:, None]])
    root = basis / np.sqrt(np.concatenate([norm, norm]))[:, None]
    wide = np.zeros((2 * N, 2 * N))
    wide[:N, 0:H], wide[:N, N : N + H] = root[:H].T, root[H:].T
    wide[N:, H:N], wide[N:, N + H :] = root[:H].T, root[H:].T
    back = np.zeros((2 * N, 2 * N))
    back[0:H, :N], back[N : N + H, :N] = basis[:H], basis[H:]
    back[H:N, N:], back[N + H :, N:] = basis[:H], basis[H:]
    offset = ((pixel + H) % N - H).astype(np.float64)
    moment = (basis * offset[None, :]) @ basis.T
    stacked = []
    for left in (root, moment):
        high, low = split_const(left)
        stacked.append(np.block([[high, high], [low, low]]))
    return np.stack([*split_const(wide), stacked[0], stacked[1], *split_const(back)])


def dot(left, right):
    return jnp.dot(left, right, preferred_element_type=F32)


def halves(values):
    high = values.astype(BF16)
    return high, (values - high.astype(F32)).astype(BF16)


def left_product(stacked, values):
    high, low = halves(values)
    both = dot(stacked, jnp.concatenate([high, low], axis=0))
    return both[:N] + both[N:]


def spectrum(pixels, wide_high, wide_low, rows):
    return left_product(rows, dot(pixels, wide_high) + dot(pixels, wide_low))


def cross(prev, cur):
    lane = lax.broadcasted_iota(jnp.int32, (H, N), 1) % H == 0

    def part(start, stop, first_row):
        def quarter(whole, row, col):
            return whole[row + start : row + stop, col : col + N]

        pcc, pcs, psc, pss = (quarter(prev, r, c) for r in (0, H) for c in (0, N))
        qcc, qcs, qsc, qss = (quarter(cur, r, c) for r in (0, H) for c in (0, N))
        edge = lane[start:stop]
        u1, u2, u3, u4 = pcc * qcc, pss * qss, pcs * qcs, psc * qsc
        v1, v2, v3, v4 = pcc * qcs, pss * qsc, pcs * qcc, psc * qss
        w1, w2, w3, w4 = pcc * qsc, pss * qcs, pcs * qss, psc * qcc
        z = pcc * qss + pss * qcc - pcs * qsc - psc * qcs
        even, odd = u2 + u3, w3 - w2
        cc = u1 + u4 + jnp.where(edge, 0.0, even)
        cs = jnp.where(edge, even, (v1 - v3) + (v4 - v2))
        sc = (w1 - w4) + jnp.where(edge, 0.0, odd)
        ss = jnp.where(edge, odd, z)
        if first_row:
            top = lax.broadcasted_iota(jnp.int32, (stop - start, N), 0) == 0
            cc = jnp.where(top, u1 + jnp.where(edge, 0.0, u3), cc)
            cs = jnp.where(top, jnp.where(edge, u3, v1 - v3), cs)
            sc = jnp.where(top, u4 + jnp.where(edge, 0.0, u2), sc)
            ss = jnp.where(top, jnp.where(edge, u2, v4 - v2), ss)
        return jnp.concatenate([cc, cs], axis=1), jnp.concatenate([sc, ss], axis=1)

    first, rest = part(0, 8, True), part(8, H, False)
    return jnp.concatenate([first[0], rest[0], first[1], rest[1]], axis=0)


def moments(prev, cur, moment, back_high, back_low):
    values = cross(prev, cur)
    along_y = jnp.sum(values * left_product(moment, values), axis=0, keepdims=True)
    along_y = along_y[:, :N] + along_y[:, N:]
    high, low = halves(values)
    pixels = dot(high, back_high) + dot(low, back_high) + dot(high, back_low)
    return along_y, jnp.sum(pixels * pixels, axis=0, keepdims=True)


def placed_flows(along_y, power, section, first_col):
    lane = lax.broadcasted_iota(jnp.int32, (8, N), 1)
    offset = ((lane + H) % N - H).astype(F32)
    pad = jnp.zeros((2, N), F32)
    flows = jnp.zeros((8, N), F32)
    stacked_y = jnp.concatenate([pad, *along_y, pad], axis=0)
    for side in range(2):
        columns = jnp.concatenate([pad, *[p[:, side * N : (side + 1) * N] for p in power], pad], axis=0)
        energy = jnp.sum(columns, axis=1, keepdims=True) * (1.0 / (N * N)) + 1e-6
        mine = (lane < H) if side == 0 else (lane >= H)
        flow_y = jnp.sum(jnp.where(mine, stacked_y, 0.0), axis=1, keepdims=True) * (1.0 / (N * N)) / energy
        flow_x = jnp.sum(columns * offset, axis=1, keepdims=True) * (1.0 / (N * N)) / energy
        slot = section * 16 + 2 + first_col + side
        flows = jnp.where(lane == slot, flow_y, flows)
        flows = jnp.where(lane == slot + 8, flow_x, flows)
    return flows


def column_flows(sums_y, sums_x, first_unit, section, first_col):
    units = range(first_unit, first_unit + 4)
    return placed_flows([sums_y[u] for u in units], [sums_x[u] for u in units], section, first_col)


def group_lanes(rows):
    return lax.broadcasted_iota(jnp.int32, (rows, N), 1) % GROUP


def edge_columns(nodes, on_right):
    lane = group_lanes(16)
    edge = jnp.zeros((16, N), F32)
    for at in range(4):
        field, to = nodes[16 * at : 16 * at + 16], EDGE * at
        side = jnp.where(on_right, pltpu.roll(field, (to - 16) % N, 1), pltpu.roll(field, (to - EDGE) % N, 1))
        edge = jnp.where((lane >= to) & (lane < to + EDGE), side, edge)
    return edge


def beside(flows, nodes, message, on_right):
    lane = lax.broadcasted_iota(jnp.int32, (8, N), 1) % 8
    left = jnp.where(lane < 2, pltpu.roll(message[:8], N - 4, 1), flows)
    right = jnp.where(lane >= 6, pltpu.roll(message[:8], 4, 1), flows)
    lane, edge = group_lanes(16), message[8:]
    first = jnp.where(on_right, EDGE + 16, 0)
    place = (lane >= first) & (lane < first + EDGE)
    fields = []
    for at in range(4):
        side = jnp.where(on_right, pltpu.roll(edge, (EDGE + 16 - EDGE * at) % N, 1), pltpu.roll(edge, -EDGE * at % N, 1))
        fields.append(jnp.where(place, side, nodes[16 * at : 16 * at + 16]))
    return jnp.where(on_right, right, left), jnp.concatenate(fields, axis=0)


def far_columns_kernel(flags_ref, own_ref, nodes_ref, far_ref, out_ref):
    flows, nodes = beside(own_ref[...], nodes_ref[...], far_ref[...] * flags_ref[1].astype(F32), flags_ref[0] == 1)
    out_ref[0:8, :] = flows
    out_ref[8:, :] = nodes


def local_kernel(flags_ref, table_hbm, patches_hbm, prior_hbm, start_hbm, weight_hbm, edges_hbm, nodes_hbm, share_hbm,
                 spec_ref, flows_ref, field_ref, far_edge_ref, near_edge_ref, table_ref, patches_ref, prior_ref, start_ref, weight_ref, edges_ref, nodes_ref, share_ref,
                 before, sums_y, sums_x, sems):
    at_start, odd = flags_ref[0] == 0, 1 - flags_ref[0]
    pairs = [(table_hbm, table_ref), (patches_hbm, patches_ref), (prior_hbm, prior_ref), (start_hbm, start_ref),
             (weight_hbm, weight_ref), (edges_hbm, edges_ref), (nodes_hbm, nodes_ref), (share_hbm, share_ref)]
    copies = [pltpu.make_async_copy(source, target, sems.at[i]) for i, (source, target) in enumerate(pairs)]
    for copy in copies:
        copy.start()
    field_ref[...] = jnp.zeros((64, N), F32)
    for copy in copies[:2]:
        copy.wait()
    forward = [table_ref[i] for i in range(3)]
    inverse = [table_ref[i] for i in range(3, 6)]
    units = [(half, py) for half in range(2) for py in range(4)]

    def pixels(ref, index, first):
        return jnp.concatenate([ref[(*index, first)], ref[(*index, first + 1)]], axis=1)

    for half, py in units:
        for section in range(2):
            spec_ref[2 * section + half, py] = spectrum(pixels(patches_ref, (section, py), 2 * (half ^ odd)), *forward)
    for copy in copies[2:]:
        copy.wait()
    for unit, (half, py) in enumerate(units):
        before[unit] = spectrum(pixels(prior_ref, (py,), 2 * (half ^ odd)), *forward)
    for unit, (half, py) in enumerate(units):
        chain = [before[unit], spec_ref[half, py], spec_ref[2 + half, py]]
        for section in range(2):
            along_y, power = moments(chain[section], chain[section + 1], *inverse)
            sums_y[8 * section + unit] = along_y
            sums_x[8 * section + unit] = power

    flows = [sum(column_flows(sums_y, sums_x, 8 * s + 4 * half, s, 2 * (half ^ odd)) for half in range(2)) for s in range(2)]
    flows_ref[...] = jnp.where(at_start, flows[0], 0.0) + flows[1]

    fields = [start_ref[s, c] for s in range(2) for c in range(2)]
    fields += [weight_ref[0], weight_ref[1], edges_ref[0].astype(F32), edges_ref[2].astype(F32)]
    fields += [nodes_ref[k].astype(F32) for k in range(4)] + [share_ref[k] for k in range(4)]
    for at, field in enumerate(fields):
        row, lane = at // 4 * 16, at % 4 * GROUP + EDGE
        field_ref[row : row + 16, lane : lane + 16] = field
    nodes = field_ref[...]
    far_edge_ref[...] = edge_columns(nodes, odd == 1)
    near_edge_ref[...] = edge_columns(nodes, odd == 0)


def middle_kernel(flags_ref, recv_ref, spec_ref, flows_ref, edge_ref, table_ref, out_ref, middle_ref, other, sums_y, sums_x):
    gz = flags_ref[0]
    forward = [table_ref[i] for i in range(3)]
    inverse = [table_ref[i] for i in range(3, 6)]
    own = 2 * (1 - gz)
    for py in range(4):
        other[py] = spectrum(jnp.concatenate([recv_ref[py, 0], recv_ref[py, 1]], axis=1), *forward)
    for py in range(4):
        mine, theirs = spec_ref[own, py], other[py]
        prev, cur = jnp.where(gz == 0, mine, theirs), jnp.where(gz == 0, theirs, mine)
        sums_y[py], sums_x[py] = moments(prev, cur, *inverse)
    flows = column_flows(sums_y, sums_x, 0, 0, 2 * (1 - gz))
    middle_ref[...] = flows
    out_ref[0:8, :] = flows_ref[...] + jnp.where(gz == 0, 0.0, flows)
    out_ref[8:, :] = edge_ref[...]


def shifted_rows(values, by):
    return pltpu.roll(values, by % values.shape[0], 0)


def nodes_kernel(flags_ref, top_ref, bottom_ref, early_ref, late_ref, spread_ref, field_ref, out_ref):
    near_on_right = flags_ref[0] == 0
    upward = flags_ref[0] == 1
    early, late = early_ref[...], late_ref[...]
    above, below = jnp.where(upward, late, early), jnp.where(upward, early, late)
    top, bottom = top_ref[...], bottom_ref[...]
    blocks = (above, top, bottom, below)
    flow_lane, lane = lax.broadcasted_iota(jnp.int32, (8, N), 1) % 8, group_lanes(8)
    flow_side = jnp.where(near_on_right, 6, 0)
    first = jnp.where(near_on_right, EDGE + 16, 0)

    def flows_of(block):
        side = jnp.where(near_on_right, pltpu.roll(block[8:16], 4, 1), pltpu.roll(block[8:16], N - 4, 1))
        return jnp.where((flow_lane >= flow_side) & (flow_lane < flow_side + 2), side, block[0:8])

    def field(at):
        rows = []
        for block in blocks:
            edge = block[48:56]
            side = jnp.where(near_on_right, pltpu.roll(edge, (EDGE + 16 - EDGE * at) % N, 1), pltpu.roll(edge, -EDGE * at % N, 1))
            rows.append(jnp.where((lane >= first) & (lane < first + EDGE), side, block[16 + 8 * at : 24 + 8 * at]))
        return jnp.concatenate(rows, axis=0)

    moved, mixed, patch, share = (field(at) for at in range(4))
    own_flows = flows_of(top)
    row = lax.broadcasted_iota(jnp.int32, (8, N), 0)
    window = jnp.where(row < 2, pltpu.roll(flows_of(above), 4, 0), jnp.where(row < 6, own_flows, pltpu.roll(flows_of(below), 4, 0)))

    narrow = window[:, : 4 * 8]
    part1 = narrow.astype(BF16)
    rest = narrow - part1.astype(F32)
    part2 = rest.astype(BF16)
    part3 = (rest - part2.astype(F32)).astype(BF16)
    spread = dot(jnp.concatenate([part1, part2, part3], axis=1), spread_ref[...])
    upper = row < 4
    lines = [[jnp.broadcast_to(spread[r : r + 1, b * N : (b + 1) * N], (8, N)) for b in range(3)] for r in range(8)]

    def patch_row(r):
        return lines[min(max(r, 0), 7)]

    rows4 = lax.broadcasted_iota(jnp.int32, (32, N), 0)
    lanes4 = lax.broadcasted_iota(jnp.int32, (32, N), 1)
    base = (1 + (rows4 + 8) % 16 // 4) * 6 + 1 + (lanes4 % GROUP + 16 - EDGE) % 16 // 4
    step = patch - base.astype(F32)

    def over_groups(values):
        values = values + pltpu.roll(values, GROUP, 1)
        return values + pltpu.roll(values, 2 * GROUP, 1)

    target = jnp.zeros((32, N), F32)
    for a in range(-1, 2):
        for b in range(-1, 2):
            weight = over_groups(jnp.where(step == float(6 * a + b), share, 0.0))
            moving = jnp.concatenate([jnp.where(upper, patch_row(2 * t + a)[b + 1], patch_row(2 * t + 1 + a)[b + 1]) for t in range(4)], axis=0)
            target = target + weight * moving

    group = lanes4 // GROUP
    stiff_pair = jnp.where(group < 2, mixed, 0.0)
    only0 = jnp.where(group == 0, mixed, 0.0)
    only1 = jnp.where(group == 1, mixed, 0.0)
    stiffness = only0 + pltpu.roll(only0, GROUP, 1) + pltpu.roll(only1, GROUP, 1) + pltpu.roll(only1, 2 * GROUP, 1)
    right = over_groups(jnp.where(group == 2, mixed, 0.0))
    down = over_groups(jnp.where(group == 3, mixed, 0.0))
    left = pltpu.roll(right, 1, 1)
    up = shifted_rows(down, 1)
    for _ in range(STEPS):
        springs = right * (pltpu.roll(moved, N - 1, 1) - moved) + left * (pltpu.roll(moved, 1, 1) - moved)
        springs = springs + down * (shifted_rows(moved, -1) - moved) + up * (shifted_rows(moved, 1) - moved)
        moved = moved + STEP_SIZE * (stiffness * (target - moved) + springs)
    for s in range(2):
        for c in range(2):
            lane = s * 16 + c * 8 + 2
            field_ref[s, c] = own_flows[2:6, lane : lane + 4]
            lane = (2 * s + c) * GROUP + EDGE
            out_ref[s, c] = moved[8:24, lane : lane + 16]


@functools.lru_cache(maxsize=None)
def spread_table():
    table = np.zeros((3, 32, 3 * N))
    for b in range(3):
        for lane in range(N):
            group, node = lane // GROUP, lane % GROUP - EDGE
            col = node // 4 + 2 + b - 1
            if 0 <= col < 8 and node < 19:
                table[:, group * 8 + col, b * N + lane] = 1.0
    return table.reshape(96, 3 * N).astype(ml_dtypes.bfloat16)


def call(kernel, inputs, out_shapes, scratch=(), flops=0, moved=0, from_hbm=()):
    from_hbm = [pltpu.with_memory_space_constraint(a, pltpu.HBM) for a in from_hbm]
    memory = [pltpu.SMEM] + [pltpu.VMEM] * (len(inputs) - 1) + [pltpu.HBM] * len(from_hbm)
    return pl.pallas_call(
        kernel,
        out_shape=out_shapes,
        in_specs=[pl.BlockSpec(memory_space=m) for m in memory],
        out_specs=jax.tree.map(lambda _: pl.BlockSpec(memory_space=pltpu.VMEM), out_shapes),
        scratch_shapes=scratch,
        compiler_params=pltpu.CompilerParams(vmem_limit_bytes=VMEM_LIMIT),
        cost_estimate=pl.CostEstimate(flops=flops, bytes_accessed=moved, transcendentals=0),
    )(*inputs, *from_hbm)


def f32(*shape):
    return jax.ShapeDtypeStruct(shape, F32)


def snake(count, forward):
    pairs = []
    for z in range(2):
        for i in range(count):
            to = i + 1 if (z == 0) == forward else i - 1
            pairs.append((z * count + i, z * count + to if 0 <= to < count else (1 - z) * count + i))
    return pairs


def body(patches, prior_patches, node_patch, node_weight, edges, flow_weight, start_offset):
    gz, gy, gx = (lax.axis_index(a) for a in ("gz", "gy", "gx"))
    rows, cols = lax.axis_size("gy"), lax.axis_size("gx")
    down = gz == 1

    def heard(place, count):
        return jnp.where(down, place < count - 1, place > 0), jnp.where(down, place > 0, place < count - 1)

    early_col, late_col = heard(gx, cols)
    early_row, late_row = (h.astype(F32) for h in heard(gy, rows))
    flags = jnp.stack([gz, early_col]).astype(jnp.int32)
    table = jnp.asarray(tables())

    chunk = lax.dynamic_slice(patches, (1 - gz, 0, 2 * gz, 0, 0), (1, 4, 2, N, N))[0]
    received = lax.ppermute(chunk, "gz", [(0, 1), (1, 0)])
    sums = [pltpu.VMEM((16, 1, N), F32), pltpu.VMEM((16, 1, 2 * N), F32)]
    arrays = [patches, prior_patches, start_offset, flow_weight, edges, node_patch, node_weight]
    spec, flows, nodes, far_edge, near_edge, table = call(
        local_kernel, [flags],
        [f32(4, 4, N, 2 * N), f32(8, N), f32(64, N), f32(16, N), f32(16, N), jax.ShapeDtypeStruct(table.shape, table.dtype)],
        [*(pltpu.VMEM(a.shape, a.dtype) for a in arrays), pltpu.VMEM((8, N, 2 * N), F32), *sums, pltpu.SemaphoreType.DMA((8,))],
        flops=8_000_000_000, moved=4_000_000, from_hbm=[table, *arrays],
    )
    to_far, middle = call(
        middle_kernel, [flags, received, spec, flows, far_edge, table],
        [f32(24, N), f32(8, N)], [pltpu.VMEM((4, N, 2 * N), F32), *sums],
        flops=2_000_000_000, moved=2_000_000,
    )
    own_middle = lax.ppermute(middle, "gz", [(0, 1), (1, 0)])
    from_far = lax.ppermute(to_far, ("gz", "gx"), snake(cols, True))
    own = to_far[:8] + own_middle * gz.astype(F32)
    from_near = lax.ppermute(jnp.concatenate([own, near_edge]), ("gz", "gx"), snake(cols, False)) * late_col.astype(F32)
    partial = call(far_columns_kernel, [flags, own, nodes, from_far], f32(72, N), flops=5_000_000_000, moved=2_000_000)

    def rows_of(first):
        return jnp.concatenate([partial[:8], from_near[:8]] + [partial[8 + 16 * f + first :][:8] for f in range(4)] + [from_near[8 + first :][:8]])

    top, bottom = rows_of(0), rows_of(8)
    row_early = lax.ppermute(jnp.where(down, top, bottom), ("gz", "gy"), snake(rows, True)) * early_row
    row_late = lax.ppermute(jnp.where(down, bottom, top), ("gz", "gy"), snake(rows, False)) * late_row
    flow_field, displacement = call(
        nodes_kernel, [flags, top, bottom, row_early, row_late, jnp.asarray(spread_table())],
        [f32(2, 2, 4, 4), f32(2, 2, 16, 16)])
    return flow_field, displacement


def solution(mesh):
    return jax.shard_map(
        body,
        mesh=mesh,
        in_specs=(
            P("gz", "gy", "gx", None, None),
            P("gy", "gx", None, None),
            P(None, "gy", "gx"),
            P(None, "gy", "gx"),
            P(None, "gy", "gx"),
            P("gz", "gy", "gx"),
            P("gz", None, "gy", "gx"),
        ),
        out_specs=(P("gz", None, "gy", "gx"), P("gz", None, "gy", "gx")),
        check_vma=False,
    )
```

```python
import functools
import math

import jax
import jax.numpy as jnp
import ml_dtypes
import numpy as np
from jax import lax
from jax.experimental import pallas as pl
from jax.experimental.pallas import tpu as pltpu
from jax.sharding import PartitionSpec as P

STEPS = 3
STEP_SIZE = 0.35
N = 128
H = N // 2
F32 = jnp.float32
BF16 = jnp.bfloat16
GROUP = 32
EDGE = 3
MOMENT_ROWS = 80
VMEM_LIMIT = 24 * 1024 * 1024


def split_const(values):
    high = values.astype(ml_dtypes.bfloat16)
    low = (values - high.astype(np.float64)).astype(ml_dtypes.bfloat16)
    return high, low


@functools.lru_cache(maxsize=None)
def tables():
    pixel = np.arange(N)
    phase = 2.0 * np.pi / N * (np.outer(np.arange(H), pixel) % N)
    cosine, sine = np.cos(phase), np.sin(phase)
    sine[0] = np.cos(np.pi * pixel)
    norm = np.full(H, math.sqrt(2.0 / N))
    norm[0] = math.sqrt(1.0 / N)
    basis = np.concatenate([cosine * norm[:, None], sine * norm[:, None]])
    root = basis / np.sqrt(np.concatenate([norm, norm]))[:, None]
    wide = np.zeros((2 * N, 2 * N))
    wide[:N, 0:H], wide[:N, N : N + H] = root[:H].T, root[H:].T
    wide[N:, H:N], wide[N:, N + H :] = root[:H].T, root[H:].T
    back = np.zeros((2 * N, 2 * N))
    back[0:H, :N], back[N : N + H, :N] = basis[:H], basis[H:]
    back[H:N, N:], back[N + H :, N:] = basis[:H], basis[H:]
    offset = ((pixel + H) % N - H).astype(np.float64)
    offset[H] = 0.0
    odd = np.zeros((MOMENT_ROWS, H))
    odd[: H + 1] = 2.0 * ((basis * offset[None, :]) @ basis.T)[: H + 1, H:]
    odd[H, 0] = 0.0
    high, low = split_const(root)
    rows = np.block([[high, high], [low, low]])
    high, low = split_const(odd)
    moment = np.zeros((2 * N, 2 * N), ml_dtypes.bfloat16)
    moment[: 2 * MOMENT_ROWS, :N] = np.block([[high, high], [low, low]])
    return np.stack([*split_const(wide), rows, moment, *split_const(back)])


def dot(left, right):
    return jnp.dot(left, right, preferred_element_type=F32)


def halves(values):
    high = values.astype(BF16)
    return high, (values - high.astype(F32)).astype(BF16)


def spectrum(pixels, wide_high, wide_low, rows):
    high, low = halves(dot(pixels, wide_high) + dot(pixels, wide_low))
    both = dot(rows, jnp.concatenate([high, low], axis=0))
    return both[:N] + both[N:]


def cross(prev, cur):
    lane = lax.broadcasted_iota(jnp.int32, (H, N), 1) % H == 0

    def part(start, stop, first_row):
        def quarter(whole, row, col):
            return whole[row + start : row + stop, col : col + N]

        pcc, pcs, psc, pss = (quarter(prev, r, c) for r in (0, H) for c in (0, N))
        qcc, qcs, qsc, qss = (quarter(cur, r, c) for r in (0, H) for c in (0, N))
        edge = lane[start:stop]
        u1, u2, u3, u4 = pcc * qcc, pss * qss, pcs * qcs, psc * qsc
        v1, v2, v3, v4 = pcc * qcs, pss * qsc, pcs * qcc, psc * qss
        w1, w2, w3, w4 = pcc * qsc, pss * qcs, pcs * qss, psc * qcc
        z = pcc * qss + pss * qcc - pcs * qsc - psc * qcs
        even, odd = u2 + u3, w3 - w2
        cc = u1 + u4 + jnp.where(edge, 0.0, even)
        cs = jnp.where(edge, even, (v1 - v3) + (v4 - v2))
        sc = (w1 - w4) + jnp.where(edge, 0.0, odd)
        ss = jnp.where(edge, odd, z)
        if first_row:
            top = lax.broadcasted_iota(jnp.int32, (stop - start, N), 0) == 0
            cc = jnp.where(top, u1 + jnp.where(edge, 0.0, u3), cc)
            cs = jnp.where(top, jnp.where(edge, u3, v1 - v3), cs)
            sc = jnp.where(top, u4 + jnp.where(edge, 0.0, u2), sc)
            ss = jnp.where(top, jnp.where(edge, u2, v4 - v2), ss)
        return jnp.concatenate([cc, cs], axis=1), jnp.concatenate([sc, ss], axis=1)

    first, rest = part(0, 8, True), part(8, H, False)
    return jnp.concatenate([first[0], rest[0], first[1], rest[1]], axis=0)


def moments(prev, cur, moment, back_high, back_low):
    values = cross(prev, cur)
    high, low = halves(values)
    both = dot(moment[: 2 * MOMENT_ROWS, :N], jnp.concatenate([high[H:], low[H:]], axis=0))
    both = both[:MOMENT_ROWS] + both[MOMENT_ROWS:]
    row = lax.broadcasted_iota(jnp.int32, (H, 2 * N), 0)
    sign = jnp.where(row == 0, math.sqrt(1.0 / N), math.sqrt(2.0 / N) * (1 - 2 * (row % 2)).astype(F32))
    halfway = jnp.sum(values[:H] * sign, axis=0, keepdims=True) + math.sqrt(1.0 / N) * values[H : H + 1]
    along_y = jnp.sum(values[:H] * both[:H], axis=0, keepdims=True) + values[H : H + 1] * both[H : H + 1] - H * halfway * halfway
    along_y = along_y[:, :N] + along_y[:, N:]
    pixels = dot(high, back_high) + dot(low, back_high) + dot(high, back_low)
    return along_y, jnp.sum(pixels * pixels, axis=0, keepdims=True)


def placed_flows(along_y, power, section, first_col):
    lane = lax.broadcasted_iota(jnp.int32, (8, N), 1)
    offset = ((lane + H) % N - H).astype(F32)
    pad = jnp.zeros((2, N), F32)
    flows = jnp.zeros((8, N), F32)
    stacked_y = jnp.concatenate([pad, *along_y, pad], axis=0)
    for side in range(2):
        columns = jnp.concatenate([pad, *[p[:, side * N : (side + 1) * N] for p in power], pad], axis=0)
        energy = jnp.sum(columns, axis=1, keepdims=True) * (1.0 / (N * N)) + 1e-6
        mine = (lane < H) if side == 0 else (lane >= H)
        flow_y = jnp.sum(jnp.where(mine, stacked_y, 0.0), axis=1, keepdims=True) * (1.0 / (N * N)) / energy
        flow_x = jnp.sum(columns * offset, axis=1, keepdims=True) * (1.0 / (N * N)) / energy
        slot = section * 16 + 2 + first_col + side
        flows = jnp.where(lane == slot, flow_y, flows)
        flows = jnp.where(lane == slot + 8, flow_x, flows)
    return flows


def column_flows(sums_y, sums_x, first_unit, section, first_col):
    units = range(first_unit, first_unit + 4)
    return placed_flows([sums_y[u] for u in units], [sums_x[u] for u in units], section, first_col)


def group_lanes(rows):
    return lax.broadcasted_iota(jnp.int32, (rows, N), 1) % GROUP


def edge_columns(nodes, on_right):
    lane = group_lanes(16)
    edge = jnp.zeros((16, N), F32)
    for at in range(4):
        field, to = nodes[16 * at : 16 * at + 16], EDGE * at
        side = jnp.where(on_right, pltpu.roll(field, (to - 16) % N, 1), pltpu.roll(field, (to - EDGE) % N, 1))
        edge = jnp.where((lane >= to) & (lane < to + EDGE), side, edge)
    return edge


def beside(flows, nodes, message, on_right):
    lane = lax.broadcasted_iota(jnp.int32, (8, N), 1) % 8
    left = jnp.where(lane < 2, pltpu.roll(message[:8], N - 4, 1), flows)
    right = jnp.where(lane >= 6, pltpu.roll(message[:8], 4, 1), flows)
    lane, edge = group_lanes(16), message[8:]
    first = jnp.where(on_right, EDGE + 16, 0)
    place = (lane >= first) & (lane < first + EDGE)
    fields = []
    for at in range(4):
        side = jnp.where(on_right, pltpu.roll(edge, (EDGE + 16 - EDGE * at) % N, 1), pltpu.roll(edge, -EDGE * at % N, 1))
        fields.append(jnp.where(place, side, nodes[16 * at : 16 * at + 16]))
    return jnp.where(on_right, right, left), jnp.concatenate(fields, axis=0)


def far_columns_kernel(flags_ref, own_ref, nodes_ref, far_ref, out_ref):
    flows, nodes = beside(own_ref[...], nodes_ref[...], far_ref[...] * flags_ref[1].astype(F32), flags_ref[0] == 1)
    out_ref[0:8, :] = flows
    out_ref[8:, :] = nodes


def local_kernel(flags_ref, table_hbm, patches_hbm, prior_hbm, start_hbm, weight_hbm, edges_hbm, nodes_hbm, share_hbm,
                 spec_ref, flows_ref, field_ref, far_edge_ref, near_edge_ref, table_ref, patches_ref, prior_ref, start_ref, weight_ref, edges_ref, nodes_ref, share_ref,
                 before, sums_y, sums_x, sems):
    at_start, odd = flags_ref[0] == 0, 1 - flags_ref[0]
    def piece(source, target, *at):
        return source.at[at], target.at[at]

    pairs = [piece(table_hbm, table_ref, pl.ds(0, 3)), piece(patches_hbm, patches_ref, 0), piece(patches_hbm, patches_ref, 1), (prior_hbm, prior_ref), piece(table_hbm, table_ref, pl.ds(3, 3)),
             (start_hbm, start_ref), (weight_hbm, weight_ref), (edges_hbm, edges_ref), (nodes_hbm, nodes_ref), (share_hbm, share_ref)]
    copies = [pltpu.make_async_copy(source, target, sems.at[i]) for i, (source, target) in enumerate(pairs)]
    for copy in copies:
        copy.start()
    field_ref[...] = jnp.zeros((64, N), F32)
    for copy in copies[:2]:
        copy.wait()
    forward = [table_ref[i] for i in range(3)]
    units = [(half, py) for half in range(2) for py in range(4)]

    def pixels(ref, index, first):
        return jnp.concatenate([ref[(*index, first)], ref[(*index, first + 1)]], axis=1)

    for section in range(2):
        for half, py in units:
            spec_ref[2 * section + half, py] = spectrum(pixels(patches_ref, (section, py), 2 * (half ^ odd)), *forward)
        if section == 0:
            for copy in copies[2:]:
                copy.wait()
    inverse = [table_ref[i] for i in range(3, 6)]
    for unit, (half, py) in enumerate(units):
        before[unit] = spectrum(pixels(prior_ref, (py,), 2 * (half ^ odd)), *forward)
    for unit, (half, py) in enumerate(units):
        chain = [before[unit], spec_ref[half, py], spec_ref[2 + half, py]]
        for section in range(2):
            along_y, power = moments(chain[section], chain[section + 1], *inverse)
            sums_y[8 * section + unit] = along_y
            sums_x[8 * section + unit] = power

    flows = [sum(column_flows(sums_y, sums_x, 8 * s + 4 * half, s, 2 * (half ^ odd)) for half in range(2)) for s in range(2)]
    flows_ref[...] = jnp.where(at_start, flows[0], 0.0) + flows[1]

    fields = [start_ref[s, c] for s in range(2) for c in range(2)]
    fields += [weight_ref[0], weight_ref[1], edges_ref[0].astype(F32), edges_ref[2].astype(F32)]
    fields += [nodes_ref[k].astype(F32) for k in range(4)] + [share_ref[k] for k in range(4)]
    for at, field in enumerate(fields):
        row, lane = at // 4 * 16, at % 4 * GROUP + EDGE
        field_ref[row : row + 16, lane : lane + 16] = field
    nodes = field_ref[...]
    far_edge_ref[...] = edge_columns(nodes, odd == 1)
    near_edge_ref[...] = edge_columns(nodes, odd == 0)


def middle_kernel(flags_ref, recv_ref, spec_ref, flows_ref, edge_ref, table_ref, out_ref, middle_ref, other, sums_y, sums_x):
    gz = flags_ref[0]
    forward = [table_ref[i] for i in range(3)]
    inverse = [table_ref[i] for i in range(3, 6)]
    own = 2 * (1 - gz)
    for py in range(4):
        other[py] = spectrum(jnp.concatenate([recv_ref[py, 0], recv_ref[py, 1]], axis=1), *forward)
    for py in range(4):
        mine, theirs = spec_ref[own, py], other[py]
        prev, cur = jnp.where(gz == 0, mine, theirs), jnp.where(gz == 0, theirs, mine)
        sums_y[py], sums_x[py] = moments(prev, cur, *inverse)
    flows = column_flows(sums_y, sums_x, 0, 0, 2 * (1 - gz))
    middle_ref[...] = flows
    out_ref[0:8, :] = flows_ref[...] + jnp.where(gz == 0, 0.0, flows)
    out_ref[8:, :] = edge_ref[...]


def shifted_rows(values, by):
    return pltpu.roll(values, by % values.shape[0], 0)


def nodes_kernel(flags_ref, top_ref, bottom_ref, early_ref, late_ref, spread_ref, field_ref, out_ref):
    near_on_right = flags_ref[0] == 0
    upward = flags_ref[0] == 1
    early, late = early_ref[...], late_ref[...]
    above, below = jnp.where(upward, late, early), jnp.where(upward, early, late)
    top, bottom = top_ref[...], bottom_ref[...]
    blocks = (above, top, bottom, below)
    flow_lane, lane = lax.broadcasted_iota(jnp.int32, (8, N), 1) % 8, group_lanes(8)
    flow_side = jnp.where(near_on_right, 6, 0)
    first = jnp.where(near_on_right, EDGE + 16, 0)

    def flows_of(block):
        side = jnp.where(near_on_right, pltpu.roll(block[8:16], 4, 1), pltpu.roll(block[8:16], N - 4, 1))
        return jnp.where((flow_lane >= flow_side) & (flow_lane < flow_side + 2), side, block[0:8])

    def field(at):
        rows = []
        for block in blocks:
            edge = block[48:56]
            side = jnp.where(near_on_right, pltpu.roll(edge, (EDGE + 16 - EDGE * at) % N, 1), pltpu.roll(edge, -EDGE * at % N, 1))
            rows.append(jnp.where((lane >= first) & (lane < first + EDGE), side, block[16 + 8 * at : 24 + 8 * at]))
        return jnp.concatenate(rows, axis=0)

    moved, mixed, patch, share = (field(at) for at in range(4))
    own_flows = flows_of(top)
    row = lax.broadcasted_iota(jnp.int32, (8, N), 0)
    window = jnp.where(row < 2, pltpu.roll(flows_of(above), 4, 0), jnp.where(row < 6, own_flows, pltpu.roll(flows_of(below), 4, 0)))

    narrow = window[:, : 4 * 8]
    part1 = narrow.astype(BF16)
    rest = narrow - part1.astype(F32)
    part2 = rest.astype(BF16)
    part3 = (rest - part2.astype(F32)).astype(BF16)
    spread = dot(jnp.concatenate([part1, part2, part3], axis=1), spread_ref[...])
    upper = row < 4
    lines = [[jnp.broadcast_to(spread[r : r + 1, b * N : (b + 1) * N], (8, N)) for b in range(3)] for r in range(8)]

    def patch_row(r):
        return lines[min(max(r, 0), 7)]

    rows4 = lax.broadcasted_iota(jnp.int32, (32, N), 0)
    lanes4 = lax.broadcasted_iota(jnp.int32, (32, N), 1)
    base = (1 + (rows4 + 8) % 16 // 4) * 6 + 1 + (lanes4 % GROUP + 16 - EDGE) % 16 // 4
    step = patch - base.astype(F32)

    def over_groups(values):
        values = values + pltpu.roll(values, GROUP, 1)
        return values + pltpu.roll(values, 2 * GROUP, 1)

    target = jnp.zeros((32, N), F32)
    for a in range(-1, 2):
        for b in range(-1, 2):
            weight = over_groups(jnp.where(step == float(6 * a + b), share, 0.0))
            moving = jnp.concatenate([jnp.where(upper, patch_row(2 * t + a)[b + 1], patch_row(2 * t + 1 + a)[b + 1]) for t in range(4)], axis=0)
            target = target + weight * moving

    group = lanes4 // GROUP
    stiff_pair = jnp.where(group < 2, mixed, 0.0)
    only0 = jnp.where(group == 0, mixed, 0.0)
    only1 = jnp.where(group == 1, mixed, 0.0)
    stiffness = only0 + pltpu.roll(only0, GROUP, 1) + pltpu.roll(only1, GROUP, 1) + pltpu.roll(only1, 2 * GROUP, 1)
    right = over_groups(jnp.where(group == 2, mixed, 0.0))
    down = over_groups(jnp.where(group == 3, mixed, 0.0))
    left = pltpu.roll(right, 1, 1)
    up = shifted_rows(down, 1)
    stay = 1.0 - STEP_SIZE * (stiffness + (right + left) + (down + up))
    pull = STEP_SIZE * stiffness * target
    right, left, down, up = (STEP_SIZE * spring for spring in (right, left, down, up))
    for _ in range(STEPS):
        across = right * pltpu.roll(moved, N - 1, 1) + left * pltpu.roll(moved, 1, 1)
        along = down * shifted_rows(moved, -1) + up * shifted_rows(moved, 1)
        moved = (stay * moved + pull) + (across + along)
    for s in range(2):
        for c in range(2):
            lane = s * 16 + c * 8 + 2
            field_ref[s, c] = own_flows[2:6, lane : lane + 4]
            lane = (2 * s + c) * GROUP + EDGE
            out_ref[s, c] = moved[8:24, lane : lane + 16]


@functools.lru_cache(maxsize=None)
def spread_table():
    table = np.zeros((3, 32, 3 * N))
    for b in range(3):
        for lane in range(N):
            group, node = lane // GROUP, lane % GROUP - EDGE
            col = node // 4 + 2 + b - 1
            if 0 <= col < 8 and node < 19:
                table[:, group * 8 + col, b * N + lane] = 1.0
    return table.reshape(96, 3 * N).astype(ml_dtypes.bfloat16)


def call(kernel, inputs, out_shapes, scratch=(), flops=0, moved=0, from_hbm=()):
    from_hbm = [pltpu.with_memory_space_constraint(a, pltpu.HBM) for a in from_hbm]
    memory = [pltpu.SMEM] + [pltpu.VMEM] * (len(inputs) - 1) + [pltpu.HBM] * len(from_hbm)
    return pl.pallas_call(
        kernel,
        out_shape=out_shapes,
        in_specs=[pl.BlockSpec(memory_space=m) for m in memory],
        out_specs=jax.tree.map(lambda _: pl.BlockSpec(memory_space=pltpu.VMEM), out_shapes),
        scratch_shapes=scratch,
        compiler_params=pltpu.CompilerParams(vmem_limit_bytes=VMEM_LIMIT),
        cost_estimate=pl.CostEstimate(flops=flops, bytes_accessed=moved, transcendentals=0),
    )(*inputs, *from_hbm)


def f32(*shape):
    return jax.ShapeDtypeStruct(shape, F32)


def snake(count, forward):
    pairs = []
    for z in range(2):
        for i in range(count):
            to = i + 1 if (z == 0) == forward else i - 1
            pairs.append((z * count + i, z * count + to if 0 <= to < count else (1 - z) * count + i))
    return pairs


def body(patches, prior_patches, node_patch, node_weight, edges, flow_weight, start_offset):
    gz, gy, gx = (lax.axis_index(a) for a in ("gz", "gy", "gx"))
    rows, cols = lax.axis_size("gy"), lax.axis_size("gx")
    down = gz == 1

    def heard(place, count):
        return jnp.where(down, place < count - 1, place > 0), jnp.where(down, place > 0, place < count - 1)

    early_col, late_col = heard(gx, cols)
    early_row, late_row = (h.astype(F32) for h in heard(gy, rows))
    flags = jnp.stack([gz, early_col]).astype(jnp.int32)
    table = jnp.asarray(tables())

    chunk = lax.dynamic_slice(patches, (1 - gz, 0, 2 * gz, 0, 0), (1, 4, 2, N, N))[0]
    received = lax.ppermute(chunk, "gz", [(0, 1), (1, 0)])
    sums = [pltpu.VMEM((16, 1, N), F32), pltpu.VMEM((16, 1, 2 * N), F32)]
    arrays = [patches, prior_patches, start_offset, flow_weight, edges, node_patch, node_weight]
    spec, flows, nodes, far_edge, near_edge, table = call(
        local_kernel, [flags],
        [f32(4, 4, N, 2 * N), f32(8, N), f32(64, N), f32(16, N), f32(16, N), jax.ShapeDtypeStruct(table.shape, table.dtype)],
        [*(pltpu.VMEM(a.shape, a.dtype) for a in arrays), pltpu.VMEM((8, N, 2 * N), F32), *sums, pltpu.SemaphoreType.DMA((10,))],
        flops=8_000_000_000, moved=4_000_000, from_hbm=[table, *arrays],
    )
    to_far, middle = call(
        middle_kernel, [flags, received, spec, flows, far_edge, table],
        [f32(24, N), f32(8, N)], [pltpu.VMEM((4, N, 2 * N), F32), *sums],
        flops=2_000_000_000, moved=2_000_000,
    )
    own_middle = lax.ppermute(middle, "gz", [(0, 1), (1, 0)])
    from_far = lax.ppermute(to_far, ("gz", "gx"), snake(cols, True))
    own = to_far[:8] + own_middle * gz.astype(F32)
    from_near = lax.ppermute(jnp.concatenate([own, near_edge]), ("gz", "gx"), snake(cols, False)) * late_col.astype(F32)
    partial = call(far_columns_kernel, [flags, own, nodes, from_far], f32(72, N), flops=5_000_000_000, moved=2_000_000)

    def rows_of(first):
        return jnp.concatenate([partial[:8], from_near[:8]] + [partial[8 + 16 * f + first :][:8] for f in range(4)] + [from_near[8 + first :][:8]])

    top, bottom = rows_of(0), rows_of(8)
    row_early = lax.ppermute(jnp.where(down, top, bottom), ("gz", "gy"), snake(rows, True)) * early_row
    row_late = lax.ppermute(jnp.where(down, bottom, top), ("gz", "gy"), snake(rows, False)) * late_row
    flow_field, displacement = call(
        nodes_kernel, [flags, top, bottom, row_early, row_late, jnp.asarray(spread_table())],
        [f32(2, 2, 4, 4), f32(2, 2, 16, 16)])
    return flow_field, displacement


def solution(mesh):
    return jax.shard_map(
        body,
        mesh=mesh,
        in_specs=(
            P("gz", "gy", "gx", None, None),
            P("gy", "gx", None, None),
            P(None, "gy", "gx"),
            P(None, "gy", "gx"),
            P(None, "gy", "gx"),
            P("gz", "gy", "gx"),
            P("gz", None, "gy", "gx"),
        ),
        out_specs=(P("gz", None, "gy", "gx"), P("gz", None, "gy", "gx")),
        check_vma=False,
    )
```

```python
import functools
import math

import jax
import jax.numpy as jnp
import ml_dtypes
import numpy as np
from jax import lax
from jax.experimental import pallas as pl
from jax.experimental.pallas import tpu as pltpu
from jax.sharding import PartitionSpec as P

STEPS = 3
STEP_SIZE = 0.35
N = 128
H = N // 2
F32 = jnp.float32
BF16 = jnp.bfloat16
GROUP = 32
EDGE = 3
MOMENT_ROWS = 80
VMEM_LIMIT = 24 * 1024 * 1024


def split_const(values):
    high = values.astype(ml_dtypes.bfloat16)
    low = (values - high.astype(np.float64)).astype(ml_dtypes.bfloat16)
    return high, low


@functools.lru_cache(maxsize=None)
def tables():
    pixel = np.arange(N)
    phase = 2.0 * np.pi / N * (np.outer(np.arange(H), pixel) % N)
    cosine, sine = np.cos(phase), np.sin(phase)
    sine[0] = np.cos(np.pi * pixel)
    norm = np.full(H, math.sqrt(2.0 / N))
    norm[0] = math.sqrt(1.0 / N)
    basis = np.concatenate([cosine * norm[:, None], sine * norm[:, None]])
    root = basis / np.sqrt(np.concatenate([norm, norm]))[:, None]
    wide = np.zeros((2 * N, 2 * N))
    wide[:N, 0:H], wide[:N, N : N + H] = root[:H].T, root[H:].T
    wide[N:, H:N], wide[N:, N + H :] = root[:H].T, root[H:].T
    back = np.zeros((2 * N, 2 * N))
    back[0:H, :N], back[N : N + H, :N] = basis[:H], basis[H:]
    back[H:N, N:], back[N + H :, N:] = basis[:H], basis[H:]
    offset = ((pixel + H) % N - H).astype(np.float64)
    offset[H] = 0.0
    odd = np.zeros((MOMENT_ROWS, H))
    odd[: H + 1] = 2.0 * ((basis * offset[None, :]) @ basis.T)[: H + 1, H:]
    odd[H, 0] = 0.0
    high, low = split_const(root)
    rows = np.block([[high, high], [low, low]])
    high, low = split_const(odd)
    moment = np.zeros((2 * N, 2 * N), ml_dtypes.bfloat16)
    moment[: 2 * MOMENT_ROWS, :N] = np.block([[high, high], [low, low]])
    return np.stack([*split_const(wide), rows, moment, *split_const(back)])


def dot(left, right):
    return jnp.dot(left, right, preferred_element_type=F32)


def halves(values):
    high = values.astype(BF16)
    return high, (values - high.astype(F32)).astype(BF16)


def spectrum(pixels, wide_high, wide_low, rows):
    high, low = halves(dot(pixels, wide_high) + dot(pixels, wide_low))
    both = dot(rows, jnp.concatenate([high, low], axis=0))
    return both[:N] + both[N:]


def cross(prev, cur):
    lane = lax.broadcasted_iota(jnp.int32, (H, N), 1) % H == 0

    def part(start, stop, first_row):
        def quarter(whole, row, col):
            return whole[row + start : row + stop, col : col + N]

        pcc, pcs, psc, pss = (quarter(prev, r, c) for r in (0, H) for c in (0, N))
        qcc, qcs, qsc, qss = (quarter(cur, r, c) for r in (0, H) for c in (0, N))
        edge = lane[start:stop]
        u1, u2, u3, u4 = pcc * qcc, pss * qss, pcs * qcs, psc * qsc
        v1, v2, v3, v4 = pcc * qcs, pss * qsc, pcs * qcc, psc * qss
        w1, w2, w3, w4 = pcc * qsc, pss * qcs, pcs * qss, psc * qcc
        z = pcc * qss + pss * qcc - pcs * qsc - psc * qcs
        even, odd = u2 + u3, w3 - w2
        cc = u1 + u4 + jnp.where(edge, 0.0, even)
        cs = jnp.where(edge, even, (v1 - v3) + (v4 - v2))
        sc = (w1 - w4) + jnp.where(edge, 0.0, odd)
        ss = jnp.where(edge, odd, z)
        if first_row:
            top = lax.broadcasted_iota(jnp.int32, (stop - start, N), 0) == 0
            cc = jnp.where(top, u1 + jnp.where(edge, 0.0, u3), cc)
            cs = jnp.where(top, jnp.where(edge, u3, v1 - v3), cs)
            sc = jnp.where(top, u4 + jnp.where(edge, 0.0, u2), sc)
            ss = jnp.where(top, jnp.where(edge, u2, v4 - v2), ss)
        return jnp.concatenate([cc, cs], axis=1), jnp.concatenate([sc, ss], axis=1)

    first, rest = part(0, 8, True), part(8, H, False)
    return jnp.concatenate([first[0], rest[0], first[1], rest[1]], axis=0)


def moments(prev, cur, moment, back_high, back_low):
    values = cross(prev, cur)
    high, low = halves(values)
    both = dot(moment[: 2 * MOMENT_ROWS, :N], jnp.concatenate([high[H:], low[H:]], axis=0))
    both = both[:MOMENT_ROWS] + both[MOMENT_ROWS:]
    row = lax.broadcasted_iota(jnp.int32, (H, 2 * N), 0)
    sign = jnp.where(row == 0, math.sqrt(1.0 / N), math.sqrt(2.0 / N) * (1 - 2 * (row % 2)).astype(F32))
    halfway = jnp.sum(values[:H] * sign, axis=0, keepdims=True) + math.sqrt(1.0 / N) * values[H : H + 1]
    along_y = jnp.sum(values[:H] * both[:H], axis=0, keepdims=True) + values[H : H + 1] * both[H : H + 1] - H * halfway * halfway
    along_y = along_y[:, :N] + along_y[:, N:]
    pixels = dot(high, back_high) + dot(low, back_high) + dot(high, back_low)
    return along_y, jnp.sum(pixels * pixels, axis=0, keepdims=True)


def placed_flows(along_y, power, section, first_col):
    lane = lax.broadcasted_iota(jnp.int32, (8, N), 1)
    offset = ((lane + H) % N - H).astype(F32)
    flows = jnp.zeros((8, N), F32)
    for side in range(2):
        columns = power[:, side * N : (side + 1) * N]
        mine = (lane < H) if side == 0 else (lane >= H)
        energy = jnp.sum(columns, axis=1, keepdims=True)
        sum_y = jnp.sum(jnp.where(mine, along_y, 0.0), axis=1, keepdims=True)
        sum_x = jnp.sum(columns * offset, axis=1, keepdims=True)
        scale = (1.0 / (N * N)) / (energy * (1.0 / (N * N)) + 1e-6)
        slot = section * 16 + 2 + first_col + side
        flows = jnp.where(lane == slot, sum_y * scale, flows)
        flows = jnp.where(lane == slot + 8, sum_x * scale, flows)
    return flows


def column_flows(sums_y, sums_x, at, section, first_col):
    return placed_flows(sums_y[at], sums_x[at], section, first_col)


def group_lanes(rows):
    return lax.broadcasted_iota(jnp.int32, (rows, N), 1) % GROUP


def edge_columns(nodes, on_right):
    lane = group_lanes(16)
    edge = jnp.zeros((16, N), F32)
    for at in range(4):
        field, to = nodes[16 * at : 16 * at + 16], EDGE * at
        side = jnp.where(on_right, pltpu.roll(field, (to - 16) % N, 1), pltpu.roll(field, (to - EDGE) % N, 1))
        edge = jnp.where((lane >= to) & (lane < to + EDGE), side, edge)
    return edge


def beside(flows, nodes, message, on_right):
    lane = lax.broadcasted_iota(jnp.int32, (8, N), 1) % 8
    left = jnp.where(lane < 2, pltpu.roll(message[:8], N - 4, 1), flows)
    right = jnp.where(lane >= 6, pltpu.roll(message[:8], 4, 1), flows)
    lane, edge = group_lanes(16), message[8:]
    first = jnp.where(on_right, EDGE + 16, 0)
    place = (lane >= first) & (lane < first + EDGE)
    fields = []
    for at in range(4):
        side = jnp.where(on_right, pltpu.roll(edge, (EDGE + 16 - EDGE * at) % N, 1), pltpu.roll(edge, -EDGE * at % N, 1))
        fields.append(jnp.where(place, side, nodes[16 * at : 16 * at + 16]))
    return jnp.where(on_right, right, left), jnp.concatenate(fields, axis=0)


def far_columns_kernel(flags_ref, own_ref, nodes_ref, far_ref, out_ref):
    flows, nodes = beside(own_ref[...], nodes_ref[...], far_ref[...] * flags_ref[1].astype(F32), flags_ref[0] == 1)
    out_ref[0:8, :] = flows
    out_ref[8:, :] = nodes


def local_kernel(flags_ref, table_hbm, patches_hbm, prior_hbm, start_hbm, weight_hbm, edges_hbm, nodes_hbm, share_hbm,
                 spec_ref, flows_ref, field_ref, far_edge_ref, near_edge_ref, table_ref, patches_ref, prior_ref, start_ref, weight_ref, edges_ref, nodes_ref, share_ref,
                 before, sums_y, sums_x, sems):
    at_start, odd = flags_ref[0] == 0, 1 - flags_ref[0]
    def piece(source, target, *at):
        return source.at[at], target.at[at]

    pairs = [piece(table_hbm, table_ref, pl.ds(0, 3)), piece(patches_hbm, patches_ref, 0), piece(patches_hbm, patches_ref, 1), (prior_hbm, prior_ref), piece(table_hbm, table_ref, pl.ds(3, 3)),
             (start_hbm, start_ref), (weight_hbm, weight_ref), (edges_hbm, edges_ref), (nodes_hbm, nodes_ref), (share_hbm, share_ref)]
    copies = [pltpu.make_async_copy(source, target, sems.at[i]) for i, (source, target) in enumerate(pairs)]
    for copy in copies:
        copy.start()
    field_ref[...] = jnp.zeros((64, N), F32)
    sums_y[...] = jnp.zeros_like(sums_y)
    sums_x[...] = jnp.zeros_like(sums_x)
    for copy in copies[:2]:
        copy.wait()
    forward = [table_ref[i] for i in range(3)]
    units = [(half, py) for half in range(2) for py in range(4)]

    def pixels(ref, index, first):
        return jnp.concatenate([ref[(*index, first)], ref[(*index, first + 1)]], axis=1)

    for section in range(2):
        for half, py in units:
            spec_ref[2 * section + half, py] = spectrum(pixels(patches_ref, (section, py), 2 * (half ^ odd)), *forward)
        if section == 0:
            for copy in copies[2:]:
                copy.wait()
    inverse = [table_ref[i] for i in range(3, 6)]
    for unit, (half, py) in enumerate(units):
        before[unit] = spectrum(pixels(prior_ref, (py,), 2 * (half ^ odd)), *forward)
    for unit, (half, py) in enumerate(units):
        chain = [before[unit], spec_ref[half, py], spec_ref[2 + half, py]]
        for section in range(2):
            along_y, power = moments(chain[section], chain[section + 1], *inverse)
            sums_y[2 * section + half, 2 + py : 3 + py, :] = along_y
            sums_x[2 * section + half, 2 + py : 3 + py, :] = power

    flows = [sum(column_flows(sums_y, sums_x, 2 * s + half, s, 2 * (half ^ odd)) for half in range(2)) for s in range(2)]
    flows_ref[...] = jnp.where(at_start, flows[0], 0.0) + flows[1]

    fields = [start_ref[s, c] for s in range(2) for c in range(2)]
    fields += [weight_ref[0], weight_ref[1], edges_ref[0].astype(F32), edges_ref[2].astype(F32)]
    fields += [nodes_ref[k].astype(F32) for k in range(4)] + [share_ref[k] for k in range(4)]
    for at, field in enumerate(fields):
        row, lane = at // 4 * 16, at % 4 * GROUP + EDGE
        field_ref[row : row + 16, lane : lane + 16] = field
    nodes = field_ref[...]
    far_edge_ref[...] = edge_columns(nodes, odd == 1)
    near_edge_ref[...] = edge_columns(nodes, odd == 0)


def middle_kernel(flags_ref, recv_ref, spec_ref, flows_ref, edge_ref, table_ref, out_ref, middle_ref, other, sums_y, sums_x):
    gz = flags_ref[0]
    forward = [table_ref[i] for i in range(3)]
    inverse = [table_ref[i] for i in range(3, 6)]
    own = 2 * (1 - gz)
    sums_y[0] = jnp.zeros((8, N), F32)
    sums_x[0] = jnp.zeros((8, 2 * N), F32)
    for py in range(4):
        other[py] = spectrum(jnp.concatenate([recv_ref[py, 0], recv_ref[py, 1]], axis=1), *forward)
    for py in range(4):
        mine, theirs = spec_ref[own, py], other[py]
        prev, cur = jnp.where(gz == 0, mine, theirs), jnp.where(gz == 0, theirs, mine)
        along_y, power = moments(prev, cur, *inverse)
        sums_y[0, 2 + py : 3 + py, :] = along_y
        sums_x[0, 2 + py : 3 + py, :] = power
    flows = column_flows(sums_y, sums_x, 0, 0, 2 * (1 - gz))
    middle_ref[...] = flows
    out_ref[0:8, :] = flows_ref[...] + jnp.where(gz == 0, 0.0, flows)
    out_ref[8:, :] = edge_ref[...]


def shifted_rows(values, by):
    return pltpu.roll(values, by % values.shape[0], 0)


def nodes_kernel(flags_ref, top_ref, bottom_ref, early_ref, late_ref, spread_ref, field_ref, out_ref):
    near_on_right = flags_ref[0] == 0
    upward = flags_ref[0] == 1
    early, late = early_ref[...], late_ref[...]
    above, below = jnp.where(upward, late, early), jnp.where(upward, early, late)
    top, bottom = top_ref[...], bottom_ref[...]
    blocks = (above, top, bottom, below)
    flow_lane, lane = lax.broadcasted_iota(jnp.int32, (8, N), 1) % 8, group_lanes(8)
    flow_side = jnp.where(near_on_right, 6, 0)
    first = jnp.where(near_on_right, EDGE + 16, 0)

    def flows_of(block):
        side = jnp.where(near_on_right, pltpu.roll(block[8:16], 4, 1), pltpu.roll(block[8:16], N - 4, 1))
        return jnp.where((flow_lane >= flow_side) & (flow_lane < flow_side + 2), side, block[0:8])

    def field(at):
        rows = []
        for block in blocks:
            edge = block[48:56]
            side = jnp.where(near_on_right, pltpu.roll(edge, (EDGE + 16 - EDGE * at) % N, 1), pltpu.roll(edge, -EDGE * at % N, 1))
            rows.append(jnp.where((lane >= first) & (lane < first + EDGE), side, block[16 + 8 * at : 24 + 8 * at]))
        return jnp.concatenate(rows, axis=0)

    moved, mixed, patch, share = (field(at) for at in range(4))
    own_flows = flows_of(top)
    row = lax.broadcasted_iota(jnp.int32, (8, N), 0)
    window = jnp.where(row < 2, pltpu.roll(flows_of(above), 4, 0), jnp.where(row < 6, own_flows, pltpu.roll(flows_of(below), 4, 0)))

    narrow = window[:, : 4 * 8]
    part1 = narrow.astype(BF16)
    rest = narrow - part1.astype(F32)
    part2 = rest.astype(BF16)
    part3 = (rest - part2.astype(F32)).astype(BF16)
    spread = dot(jnp.concatenate([part1, part2, part3], axis=1), spread_ref[...])
    upper = row < 4
    lines = [[jnp.broadcast_to(spread[r : r + 1, b * N : (b + 1) * N], (8, N)) for b in range(3)] for r in range(8)]

    def patch_row(r):
        return lines[min(max(r, 0), 7)]

    rows4 = lax.broadcasted_iota(jnp.int32, (32, N), 0)
    lanes4 = lax.broadcasted_iota(jnp.int32, (32, N), 1)
    base = (1 + (rows4 + 8) % 16 // 4) * 6 + 1 + (lanes4 % GROUP + 16 - EDGE) % 16 // 4
    step = patch - base.astype(F32)

    def over_groups(values):
        values = values + pltpu.roll(values, GROUP, 1)
        return values + pltpu.roll(values, 2 * GROUP, 1)

    target = jnp.zeros((32, N), F32)
    for a in range(-1, 2):
        for b in range(-1, 2):
            weight = over_groups(jnp.where(step == float(6 * a + b), share, 0.0))
            moving = jnp.concatenate([jnp.where(upper, patch_row(2 * t + a)[b + 1], patch_row(2 * t + 1 + a)[b + 1]) for t in range(4)], axis=0)
            target = target + weight * moving

    group = lanes4 // GROUP
    stiff_pair = jnp.where(group < 2, mixed, 0.0)
    only0 = jnp.where(group == 0, mixed, 0.0)
    only1 = jnp.where(group == 1, mixed, 0.0)
    stiffness = only0 + pltpu.roll(only0, GROUP, 1) + pltpu.roll(only1, GROUP, 1) + pltpu.roll(only1, 2 * GROUP, 1)
    right = over_groups(jnp.where(group == 2, mixed, 0.0))
    down = over_groups(jnp.where(group == 3, mixed, 0.0))
    left = pltpu.roll(right, 1, 1)
    up = shifted_rows(down, 1)
    stay = 1.0 - STEP_SIZE * (stiffness + (right + left) + (down + up))
    pull = STEP_SIZE * stiffness * target
    right, left, down, up = (STEP_SIZE * spring for spring in (right, left, down, up))
    for _ in range(STEPS):
        across = right * pltpu.roll(moved, N - 1, 1) + left * pltpu.roll(moved, 1, 1)
        along = down * shifted_rows(moved, -1) + up * shifted_rows(moved, 1)
        moved = (stay * moved + pull) + (across + along)
    for s in range(2):
        for c in range(2):
            lane = s * 16 + c * 8 + 2
            field_ref[s, c] = own_flows[2:6, lane : lane + 4]
            lane = (2 * s + c) * GROUP + EDGE
            out_ref[s, c] = moved[8:24, lane : lane + 16]


@functools.lru_cache(maxsize=None)
def spread_table():
    table = np.zeros((3, 32, 3 * N))
    for b in range(3):
        for lane in range(N):
            group, node = lane // GROUP, lane % GROUP - EDGE
            col = node // 4 + 2 + b - 1
            if 0 <= col < 8 and node < 19:
                table[:, group * 8 + col, b * N + lane] = 1.0
    return table.reshape(96, 3 * N).astype(ml_dtypes.bfloat16)


def call(kernel, inputs, out_shapes, scratch=(), flops=0, moved=0, from_hbm=()):
    from_hbm = [pltpu.with_memory_space_constraint(a, pltpu.HBM) for a in from_hbm]
    memory = [pltpu.SMEM] + [pltpu.VMEM] * (len(inputs) - 1) + [pltpu.HBM] * len(from_hbm)
    return pl.pallas_call(
        kernel,
        out_shape=out_shapes,
        in_specs=[pl.BlockSpec(memory_space=m) for m in memory],
        out_specs=jax.tree.map(lambda _: pl.BlockSpec(memory_space=pltpu.VMEM), out_shapes),
        scratch_shapes=scratch,
        compiler_params=pltpu.CompilerParams(vmem_limit_bytes=VMEM_LIMIT),
        cost_estimate=pl.CostEstimate(flops=flops, bytes_accessed=moved, transcendentals=0),
    )(*inputs, *from_hbm)


def f32(*shape):
    return jax.ShapeDtypeStruct(shape, F32)


def snake(count, forward):
    pairs = []
    for z in range(2):
        for i in range(count):
            to = i + 1 if (z == 0) == forward else i - 1
            pairs.append((z * count + i, z * count + to if 0 <= to < count else (1 - z) * count + i))
    return pairs


def body(patches, prior_patches, node_patch, node_weight, edges, flow_weight, start_offset):
    gz, gy, gx = (lax.axis_index(a) for a in ("gz", "gy", "gx"))
    rows, cols = lax.axis_size("gy"), lax.axis_size("gx")
    down = gz == 1

    def heard(place, count):
        return jnp.where(down, place < count - 1, place > 0), jnp.where(down, place > 0, place < count - 1)

    early_col, late_col = heard(gx, cols)
    early_row, late_row = (h.astype(F32) for h in heard(gy, rows))
    flags = jnp.stack([gz, early_col]).astype(jnp.int32)
    table = jnp.asarray(tables())

    chunk = lax.dynamic_slice(patches, (1 - gz, 0, 2 * gz, 0, 0), (1, 4, 2, N, N))[0]
    received = lax.ppermute(chunk, "gz", [(0, 1), (1, 0)])
    sums = [pltpu.VMEM((4, 8, N), F32), pltpu.VMEM((4, 8, 2 * N), F32)]
    arrays = [patches, prior_patches, start_offset, flow_weight, edges, node_patch, node_weight]
    spec, flows, nodes, far_edge, near_edge, table = call(
        local_kernel, [flags],
        [f32(4, 4, N, 2 * N), f32(8, N), f32(64, N), f32(16, N), f32(16, N), jax.ShapeDtypeStruct(table.shape, table.dtype)],
        [*(pltpu.VMEM(a.shape, a.dtype) for a in arrays), pltpu.VMEM((8, N, 2 * N), F32), *sums, pltpu.SemaphoreType.DMA((10,))],
        flops=8_000_000_000, moved=4_000_000, from_hbm=[table, *arrays],
    )
    to_far, middle = call(
        middle_kernel, [flags, received, spec, flows, far_edge, table],
        [f32(24, N), f32(8, N)], [pltpu.VMEM((4, N, 2 * N), F32), *sums],
        flops=2_000_000_000, moved=2_000_000,
    )
    own_middle = lax.ppermute(middle, "gz", [(0, 1), (1, 0)])
    from_far = lax.ppermute(to_far, ("gz", "gx"), snake(cols, True))
    own = to_far[:8] + own_middle * gz.astype(F32)
    from_near = lax.ppermute(jnp.concatenate([own, near_edge]), ("gz", "gx"), snake(cols, False)) * late_col.astype(F32)
    partial = call(far_columns_kernel, [flags, own, nodes, from_far], f32(72, N), flops=5_000_000_000, moved=2_000_000)

    def rows_of(first):
        return jnp.concatenate([partial[:8], from_near[:8]] + [partial[8 + 16 * f + first :][:8] for f in range(4)] + [from_near[8 + first :][:8]])

    top, bottom = rows_of(0), rows_of(8)
    row_early = lax.ppermute(jnp.where(down, top, bottom), ("gz", "gy"), snake(rows, True)) * early_row
    row_late = lax.ppermute(jnp.where(down, bottom, top), ("gz", "gy"), snake(rows, False)) * late_row
    flow_field, displacement = call(
        nodes_kernel, [flags, top, bottom, row_early, row_late, jnp.asarray(spread_table())],
        [f32(2, 2, 4, 4), f32(2, 2, 16, 16)])
    return flow_field, displacement


def solution(mesh):
    return jax.shard_map(
        body,
        mesh=mesh,
        in_specs=(
            P("gz", "gy", "gx", None, None),
            P("gy", "gx", None, None),
            P(None, "gy", "gx"),
            P(None, "gy", "gx"),
            P(None, "gy", "gx"),
            P("gz", "gy", "gx"),
            P("gz", None, "gy", "gx"),
        ),
        out_specs=(P("gz", None, "gy", "gx"), P("gz", None, "gy", "gx")),
        check_vma=False,
    )
```

```python
import functools
import math

import jax
import jax.numpy as jnp
import ml_dtypes
import numpy as np
from jax import lax
from jax.experimental import pallas as pl
from jax.experimental.pallas import tpu as pltpu
from jax.sharding import PartitionSpec as P

STEPS = 3
STEP_SIZE = 0.35
N = 128
H = N // 2
F32 = jnp.float32
BF16 = jnp.bfloat16
GROUP = 32
EDGE = 3
MOMENT_ROWS = 80
VMEM_LIMIT = 24 * 1024 * 1024


def split_const(values):
    high = values.astype(ml_dtypes.bfloat16)
    low = (values - high.astype(np.float64)).astype(ml_dtypes.bfloat16)
    return high, low


@functools.lru_cache(maxsize=None)
def tables():
    pixel = np.arange(N)
    phase = 2.0 * np.pi / N * (np.outer(np.arange(H), pixel) % N)
    cosine, sine = np.cos(phase), np.sin(phase)
    sine[0] = np.cos(np.pi * pixel)
    norm = np.full(H, math.sqrt(2.0 / N))
    norm[0] = math.sqrt(1.0 / N)
    basis = np.concatenate([cosine * norm[:, None], sine * norm[:, None]])
    root = basis / np.sqrt(np.concatenate([norm, norm]))[:, None]
    wide = np.zeros((2 * N, 2 * N))
    wide[:N, 0:H], wide[:N, N : N + H] = root[:H].T, root[H:].T
    wide[N:, H:N], wide[N:, N + H :] = root[:H].T, root[H:].T
    back = np.zeros((2 * N, 2 * N))
    back[0:H, :N], back[N : N + H, :N] = basis[:H], basis[H:]
    back[H:N, N:], back[N + H :, N:] = basis[:H], basis[H:]
    offset = ((pixel + H) % N - H).astype(np.float64)
    offset[H] = 0.0
    odd = np.zeros((MOMENT_ROWS, H))
    odd[: H + 1] = 2.0 * ((basis * offset[None, :]) @ basis.T)[: H + 1, H:]
    odd[H, 0] = 0.0
    high, low = split_const(root)
    rows = np.block([[high, high], [low, low]])
    high, low = split_const(odd)
    moment = np.zeros((2 * N, 2 * N), ml_dtypes.bfloat16)
    moment[: 2 * MOMENT_ROWS, :N] = np.block([[high, high], [low, low]])
    return np.stack([*split_const(wide), rows, moment, *split_const(back)])


def dot(left, right):
    return jnp.dot(left, right, preferred_element_type=F32)


def halves(values):
    high = values.astype(BF16)
    return high, (values - high.astype(F32)).astype(BF16)


def spectrum(pixels, wide_high, wide_low, rows):
    high, low = halves(dot(pixels, wide_high) + dot(pixels, wide_low))
    both = dot(rows, jnp.concatenate([high, low], axis=0))
    return both[:N] + both[N:]


def cross(prev, cur):
    lane = lax.broadcasted_iota(jnp.int32, (H, N), 1) % H == 0

    def part(start, stop, first_row):
        def quarter(whole, row, col):
            return whole[row + start : row + stop, col : col + N]

        pcc, pcs, psc, pss = (quarter(prev, r, c) for r in (0, H) for c in (0, N))
        qcc, qcs, qsc, qss = (quarter(cur, r, c) for r in (0, H) for c in (0, N))
        edge = lane[start:stop]
        u1, u2, u3, u4 = pcc * qcc, pss * qss, pcs * qcs, psc * qsc
        v1, v2, v3, v4 = pcc * qcs, pss * qsc, pcs * qcc, psc * qss
        w1, w2, w3, w4 = pcc * qsc, pss * qcs, pcs * qss, psc * qcc
        z = pcc * qss + pss * qcc - pcs * qsc - psc * qcs
        even, odd = u2 + u3, w3 - w2
        cc = u1 + u4 + jnp.where(edge, 0.0, even)
        cs = jnp.where(edge, even, (v1 - v3) + (v4 - v2))
        sc = (w1 - w4) + jnp.where(edge, 0.0, odd)
        ss = jnp.where(edge, odd, z)
        if first_row:
            top = lax.broadcasted_iota(jnp.int32, (stop - start, N), 0) == 0
            cc = jnp.where(top, u1 + jnp.where(edge, 0.0, u3), cc)
            cs = jnp.where(top, jnp.where(edge, u3, v1 - v3), cs)
            sc = jnp.where(top, u4 + jnp.where(edge, 0.0, u2), sc)
            ss = jnp.where(top, jnp.where(edge, u2, v4 - v2), ss)
        return jnp.concatenate([cc, cs], axis=1), jnp.concatenate([sc, ss], axis=1)

    first, rest = part(0, 8, True), part(8, H, False)
    return jnp.concatenate([first[0], rest[0], first[1], rest[1]], axis=0)


def moments(prev, cur, moment, back_high, back_low):
    values = cross(prev, cur)
    high, low = halves(values)
    both = dot(moment[: 2 * MOMENT_ROWS, :N], jnp.concatenate([high[H:], low[H:]], axis=0))
    both = both[:MOMENT_ROWS] + both[MOMENT_ROWS:]
    row = lax.broadcasted_iota(jnp.int32, (H, 2 * N), 0)
    sign = jnp.where(row == 0, math.sqrt(1.0 / N), math.sqrt(2.0 / N) * (1 - 2 * (row % 2)).astype(F32))
    halfway = jnp.sum(values[:H] * sign, axis=0, keepdims=True) + math.sqrt(1.0 / N) * values[H : H + 1]
    along_y = jnp.sum(values[:H] * both[:H], axis=0, keepdims=True) + values[H : H + 1] * both[H : H + 1] - H * halfway * halfway
    along_y = along_y[:, :N] + along_y[:, N:]
    pixels = dot(high, back_high) + dot(low, back_high) + dot(high, back_low)
    return along_y, jnp.sum(pixels * pixels, axis=0, keepdims=True)


def placed_flows(along_y, power, section, first_col):
    lane = lax.broadcasted_iota(jnp.int32, (8, N), 1)
    offset = ((lane + H) % N - H).astype(F32)
    flows = jnp.zeros((8, N), F32)
    for side in range(2):
        columns = power[:, side * N : (side + 1) * N]
        mine = (lane < H) if side == 0 else (lane >= H)
        energy = jnp.sum(columns, axis=1, keepdims=True)
        sum_y = jnp.sum(jnp.where(mine, along_y, 0.0), axis=1, keepdims=True)
        sum_x = jnp.sum(columns * offset, axis=1, keepdims=True)
        scale = (1.0 / (N * N)) / (energy * (1.0 / (N * N)) + 1e-6)
        slot = section * 16 + 2 + first_col + side
        flows = jnp.where(lane == slot, sum_y * scale, flows)
        flows = jnp.where(lane == slot + 8, sum_x * scale, flows)
    return flows


def column_flows(sums_y, sums_x, at, section, first_col):
    return placed_flows(sums_y[at], sums_x[at], section, first_col)


def group_lanes(rows):
    return lax.broadcasted_iota(jnp.int32, (rows, N), 1) % GROUP


def edge_columns(nodes, on_right):
    lane = group_lanes(16)
    edge = jnp.zeros((16, N), F32)
    for at in range(4):
        field, to = nodes[16 * at : 16 * at + 16], EDGE * at
        side = jnp.where(on_right, pltpu.roll(field, (to - 16) % N, 1), pltpu.roll(field, (to - EDGE) % N, 1))
        edge = jnp.where((lane >= to) & (lane < to + EDGE), side, edge)
    return edge


def beside(flows, nodes, message, on_right):
    lane = lax.broadcasted_iota(jnp.int32, (8, N), 1) % 8
    left = jnp.where(lane < 2, pltpu.roll(message[:8], N - 4, 1), flows)
    right = jnp.where(lane >= 6, pltpu.roll(message[:8], 4, 1), flows)
    lane, edge = group_lanes(16), message[8:]
    first = jnp.where(on_right, EDGE + 16, 0)
    place = (lane >= first) & (lane < first + EDGE)
    fields = []
    for at in range(4):
        side = jnp.where(on_right, pltpu.roll(edge, (EDGE + 16 - EDGE * at) % N, 1), pltpu.roll(edge, -EDGE * at % N, 1))
        fields.append(jnp.where(place, side, nodes[16 * at : 16 * at + 16]))
    return jnp.where(on_right, right, left), jnp.concatenate(fields, axis=0)


def far_columns_kernel(flags_ref, own_ref, nodes_ref, far_ref, out_ref):
    flows, nodes = beside(own_ref[...], nodes_ref[...], far_ref[...] * flags_ref[1].astype(F32), flags_ref[0] == 1)
    out_ref[0:8, :] = flows
    out_ref[8:, :] = nodes


def local_kernel(flags_ref, table_hbm, patches_hbm, prior_hbm, start_hbm, weight_hbm, edges_hbm, nodes_hbm, share_hbm,
                 spec_ref, flows_ref, field_ref, far_edge_ref, near_edge_ref, table_ref, patches_ref, prior_ref, start_ref, weight_ref, edges_ref, nodes_ref, share_ref,
                 before, sums_y, sums_x, sems):
    at_start, odd = flags_ref[0] == 0, 1 - flags_ref[0]
    def piece(source, target, *at):
        return source.at[at], target.at[at]

    pairs = [piece(table_hbm, table_ref, pl.ds(0, 3)), piece(patches_hbm, patches_ref, 0), piece(patches_hbm, patches_ref, 1), (prior_hbm, prior_ref), piece(table_hbm, table_ref, pl.ds(3, 3)),
             (start_hbm, start_ref), (weight_hbm, weight_ref), (edges_hbm, edges_ref), (nodes_hbm, nodes_ref), (share_hbm, share_ref)]
    copies = [pltpu.make_async_copy(source, target, sems.at[i]) for i, (source, target) in enumerate(pairs)]
    for copy in copies:
        copy.start()
    field_ref[...] = jnp.zeros((64, N), F32)
    sums_y[...] = jnp.zeros_like(sums_y)
    sums_x[...] = jnp.zeros_like(sums_x)
    for copy in copies[:2]:
        copy.wait()
    forward = [table_ref[i] for i in range(3)]
    units = [(half, py) for half in range(2) for py in range(4)]

    def pixels(ref, index, first):
        return jnp.concatenate([ref[(*index, first)], ref[(*index, first + 1)]], axis=1)

    for section in range(2):
        for half, py in units:
            spec_ref[2 * section + half, py] = spectrum(pixels(patches_ref, (section, py), 2 * (half ^ odd)), *forward)
        if section == 0:
            for copy in copies[2:]:
                copy.wait()
    inverse = [table_ref[i] for i in range(3, 6)]
    for unit, (half, py) in enumerate(units):
        before[unit] = spectrum(pixels(prior_ref, (py,), 2 * (half ^ odd)), *forward)
    for unit, (half, py) in enumerate(units):
        chain = [before[unit], spec_ref[half, py], spec_ref[2 + half, py]]
        for section in range(2):
            along_y, power = moments(chain[section], chain[section + 1], *inverse)
            sums_y[2 * section + half, 2 + py : 3 + py, :] = along_y
            sums_x[2 * section + half, 2 + py : 3 + py, :] = power

    flows = [sum(column_flows(sums_y, sums_x, 2 * s + half, s, 2 * (half ^ odd)) for half in range(2)) for s in range(2)]
    flows_ref[...] = jnp.where(at_start, flows[0], 0.0) + flows[1]

    fields = [start_ref[s, c] for s in range(2) for c in range(2)]
    fields += [weight_ref[0], weight_ref[1], edges_ref[0].astype(F32), edges_ref[2].astype(F32)]
    fields += [nodes_ref[k].astype(F32) for k in range(4)] + [share_ref[k] for k in range(4)]
    for at, field in enumerate(fields):
        row, lane = at // 4 * 16, at % 4 * GROUP + EDGE
        field_ref[row : row + 16, lane : lane + 16] = field
    nodes = field_ref[...]
    far_edge_ref[...] = edge_columns(nodes, odd == 1)
    near_edge_ref[...] = edge_columns(nodes, odd == 0)


def middle_kernel(flags_ref, recv_ref, spec_ref, flows_ref, edge_ref, table_ref, out_ref, middle_ref, other, sums_y, sums_x):
    gz = flags_ref[0]
    forward = [table_ref[i] for i in range(3)]
    inverse = [table_ref[i] for i in range(3, 6)]
    own = 2 * (1 - gz)
    sums_y[0] = jnp.zeros((8, N), F32)
    sums_x[0] = jnp.zeros((8, 2 * N), F32)
    for py in range(4):
        other[py] = spectrum(jnp.concatenate([recv_ref[py, 0], recv_ref[py, 1]], axis=1), *forward)
    for py in range(4):
        mine, theirs = spec_ref[own, py], other[py]
        prev, cur = jnp.where(gz == 0, mine, theirs), jnp.where(gz == 0, theirs, mine)
        along_y, power = moments(prev, cur, *inverse)
        sums_y[0, 2 + py : 3 + py, :] = along_y
        sums_x[0, 2 + py : 3 + py, :] = power
    flows = column_flows(sums_y, sums_x, 0, 0, 2 * (1 - gz))
    middle_ref[...] = flows
    out_ref[0:8, :] = flows_ref[...] + jnp.where(gz == 0, 0.0, flows)
    out_ref[8:, :] = edge_ref[...]


def shifted_rows(values, by):
    return pltpu.roll(values, by % values.shape[0], 0)


def nodes_kernel(flags_ref, top_ref, bottom_ref, early_ref, late_ref, spread_ref, field_ref, out_ref):
    near_on_right = flags_ref[0] == 0
    upward = flags_ref[0] == 1
    early, late = early_ref[...], late_ref[...]
    above, below = jnp.where(upward, late, early), jnp.where(upward, early, late)
    top, bottom = top_ref[...], bottom_ref[...]
    blocks = (above, top, bottom, below)
    flow_lane, lane = lax.broadcasted_iota(jnp.int32, (8, N), 1) % 8, group_lanes(8)
    flow_side = jnp.where(near_on_right, 6, 0)
    first = jnp.where(near_on_right, EDGE + 16, 0)

    def flows_of(block):
        side = jnp.where(near_on_right, pltpu.roll(block[8:16], 4, 1), pltpu.roll(block[8:16], N - 4, 1))
        return jnp.where((flow_lane >= flow_side) & (flow_lane < flow_side + 2), side, block[0:8])

    def field(at):
        rows = []
        for block in blocks:
            edge = block[48:56]
            side = pltpu.roll(edge, jnp.where(near_on_right, (EDGE + 16 - EDGE * at) % N, -EDGE * at % N), 1)
            rows.append(jnp.where((lane >= first) & (lane < first + EDGE), side, block[16 + 8 * at : 24 + 8 * at]))
        return jnp.concatenate(rows, axis=0)

    moved, mixed, patch, share = (field(at) for at in range(4))
    own_flows = flows_of(top)
    row = lax.broadcasted_iota(jnp.int32, (8, N), 0)
    window = jnp.where(row < 2, pltpu.roll(flows_of(above), 4, 0), jnp.where(row < 6, own_flows, pltpu.roll(flows_of(below), 4, 0)))

    narrow = window[:, : 4 * 8]
    spread = dot(jnp.concatenate(halves(narrow), axis=1), spread_ref[...])
    upper = row < 4
    lines = [[jnp.broadcast_to(spread[r : r + 1, b * N : (b + 1) * N], (8, N)) for b in range(3)] for r in range(8)]

    def patch_row(r):
        return lines[min(max(r, 0), 7)]

    rows4 = lax.broadcasted_iota(jnp.int32, (32, N), 0)
    lanes4 = lax.broadcasted_iota(jnp.int32, (32, N), 1)
    base = (1 + (rows4 + 8) % 16 // 4) * 6 + 1 + (lanes4 % GROUP + 16 - EDGE) % 16 // 4
    step = patch - base.astype(F32)

    def over_groups(values):
        values = values + pltpu.roll(values, GROUP, 1)
        return values + pltpu.roll(values, 2 * GROUP, 1)

    target = jnp.zeros((32, N), F32)
    for a in range(-1, 2):
        for b in range(-1, 2):
            weight = over_groups(jnp.where(step == float(6 * a + b), share, 0.0))
            moving = jnp.concatenate([jnp.where(upper, patch_row(2 * t + a)[b + 1], patch_row(2 * t + 1 + a)[b + 1]) for t in range(4)], axis=0)
            target = target + weight * moving

    group = lanes4 // GROUP
    stiff_pair = jnp.where(group < 2, mixed, 0.0)
    only0 = jnp.where(group == 0, mixed, 0.0)
    only1 = jnp.where(group == 1, mixed, 0.0)
    stiffness = only0 + pltpu.roll(only0, GROUP, 1) + pltpu.roll(only1, GROUP, 1) + pltpu.roll(only1, 2 * GROUP, 1)
    right = over_groups(jnp.where(group == 2, mixed, 0.0))
    down = over_groups(jnp.where(group == 3, mixed, 0.0))
    left = pltpu.roll(right, 1, 1)
    up = shifted_rows(down, 1)
    stay = 1.0 - STEP_SIZE * (stiffness + (right + left) + (down + up))
    pull = STEP_SIZE * stiffness * target
    right, left, down, up = (STEP_SIZE * spring for spring in (right, left, down, up))
    for _ in range(STEPS):
        across = right * pltpu.roll(moved, N - 1, 1) + left * pltpu.roll(moved, 1, 1)
        along = down * shifted_rows(moved, -1) + up * shifted_rows(moved, 1)
        moved = (stay * moved + pull) + (across + along)
    for s in range(2):
        for c in range(2):
            lane = s * 16 + c * 8 + 2
            field_ref[s, c] = own_flows[2:6, lane : lane + 4]
            lane = (2 * s + c) * GROUP + EDGE
            out_ref[s, c] = moved[8:24, lane : lane + 16]


@functools.lru_cache(maxsize=None)
def spread_table():
    table = np.zeros((2, 32, 3 * N))
    for b in range(3):
        for lane in range(N):
            group, node = lane // GROUP, lane % GROUP - EDGE
            col = node // 4 + 2 + b - 1
            if 0 <= col < 8 and node < 19:
                table[:, group * 8 + col, b * N + lane] = 1.0
    return table.reshape(64, 3 * N).astype(ml_dtypes.bfloat16)


def call(kernel, inputs, out_shapes, scratch=(), flops=0, moved=0, from_hbm=()):
    from_hbm = [pltpu.with_memory_space_constraint(a, pltpu.HBM) for a in from_hbm]
    memory = [pltpu.SMEM] + [pltpu.VMEM] * (len(inputs) - 1) + [pltpu.HBM] * len(from_hbm)
    return pl.pallas_call(
        kernel,
        out_shape=out_shapes,
        in_specs=[pl.BlockSpec(memory_space=m) for m in memory],
        out_specs=jax.tree.map(lambda _: pl.BlockSpec(memory_space=pltpu.VMEM), out_shapes),
        scratch_shapes=scratch,
        compiler_params=pltpu.CompilerParams(vmem_limit_bytes=VMEM_LIMIT),
        cost_estimate=pl.CostEstimate(flops=flops, bytes_accessed=moved, transcendentals=0),
    )(*inputs, *from_hbm)


def f32(*shape):
    return jax.ShapeDtypeStruct(shape, F32)


def snake(count, forward):
    pairs = []
    for z in range(2):
        for i in range(count):
            to = i + 1 if (z == 0) == forward else i - 1
            pairs.append((z * count + i, z * count + to if 0 <= to < count else (1 - z) * count + i))
    return pairs


def body(patches, prior_patches, node_patch, node_weight, edges, flow_weight, start_offset):
    gz, gy, gx = (lax.axis_index(a) for a in ("gz", "gy", "gx"))
    rows, cols = lax.axis_size("gy"), lax.axis_size("gx")
    down = gz == 1

    def heard(place, count):
        return jnp.where(down, place < count - 1, place > 0), jnp.where(down, place > 0, place < count - 1)

    early_col, late_col = heard(gx, cols)
    early_row, late_row = (h.astype(F32) for h in heard(gy, rows))
    flags = jnp.stack([gz, early_col]).astype(jnp.int32)
    table = jnp.asarray(tables())

    chunk = lax.dynamic_slice(patches, (1 - gz, 0, 2 * gz, 0, 0), (1, 4, 2, N, N))[0]
    received = lax.ppermute(chunk, "gz", [(0, 1), (1, 0)])
    sums = [pltpu.VMEM((4, 8, N), F32), pltpu.VMEM((4, 8, 2 * N), F32)]
    arrays = [patches, prior_patches, start_offset, flow_weight, edges, node_patch, node_weight]
    spec, flows, nodes, far_edge, near_edge, table = call(
        local_kernel, [flags],
        [f32(4, 4, N, 2 * N), f32(8, N), f32(64, N), f32(16, N), f32(16, N), jax.ShapeDtypeStruct(table.shape, table.dtype)],
        [*(pltpu.VMEM(a.shape, a.dtype) for a in arrays), pltpu.VMEM((8, N, 2 * N), F32), *sums, pltpu.SemaphoreType.DMA((10,))],
        flops=8_000_000_000, moved=4_000_000, from_hbm=[table, *arrays],
    )
    to_far, middle = call(
        middle_kernel, [flags, received, spec, flows, far_edge, table],
        [f32(24, N), f32(8, N)], [pltpu.VMEM((4, N, 2 * N), F32), *sums],
        flops=2_000_000_000, moved=2_000_000,
    )
    own_middle = lax.ppermute(middle, "gz", [(0, 1), (1, 0)])
    from_far = lax.ppermute(to_far, ("gz", "gx"), snake(cols, True))
    own = to_far[:8] + own_middle * gz.astype(F32)
    from_near = lax.ppermute(jnp.concatenate([own, near_edge]), ("gz", "gx"), snake(cols, False)) * late_col.astype(F32)
    partial = call(far_columns_kernel, [flags, own, nodes, from_far], f32(72, N), flops=5_000_000_000, moved=2_000_000)

    def rows_of(first):
        return jnp.concatenate([partial[:8], from_near[:8]] + [partial[8 + 16 * f + first :][:8] for f in range(4)] + [from_near[8 + first :][:8]])

    top, bottom = rows_of(0), rows_of(8)
    row_early = lax.ppermute(jnp.where(down, top, bottom), ("gz", "gy"), snake(rows, True)) * early_row
    row_late = lax.ppermute(jnp.where(down, bottom, top), ("gz", "gy"), snake(rows, False)) * late_row
    flow_field, displacement = call(
        nodes_kernel, [flags, top, bottom, row_early, row_late, jnp.asarray(spread_table())],
        [f32(2, 2, 4, 4), f32(2, 2, 16, 16)])
    return flow_field, displacement


def solution(mesh):
    return jax.shard_map(
        body,
        mesh=mesh,
        in_specs=(
            P("gz", "gy", "gx", None, None),
            P("gy", "gx", None, None),
            P(None, "gy", "gx"),
            P(None, "gy", "gx"),
            P(None, "gy", "gx"),
            P("gz", "gy", "gx"),
            P("gz", None, "gy", "gx"),
        ),
        out_specs=(P("gz", None, "gy", "gx"), P("gz", None, "gy", "gx")),
        check_vma=False,
    )
```
